256 devices in a mesh: comp: 32 (over y, x, core), tile: 8 (over z).
Axes of the slice: x: 4, y: 4, z: 8, core: 2. Of those that a mesh axis runs over, the one named last changes fastest.
Arguments:
- spectrum: float32 [864, 256, 512], P('comp', 'tile'), may hold values from 0.1 to 2
- speed: float32 [864], P('comp'), may hold values from 0.2 to 0.7
- depth: float32 [256, 512], P('tile'), may hold values from 0.5 to 1.2
- turn: float32 [256, 512], P('tile'), may hold values from -4 to 4
- sea_mask: int32 [256, 512], P('tile'), may hold values from 0 to 1, as said below
- refraction: float32 [24], replicated, may hold values from 0.1 to 0.6
- growth: float32 [864], replicated, may hold values from 0.1 to 1
- dissipation: float32 [864], replicated, may hold values from 0.1 to 1
- quad_first: bfloat16 [864, 864], replicated, may hold values from -0.21875 to 0.21875
- quad_second: bfloat16 [864, 864], replicated, may hold values from -0.21875 to 0.21875
Outputs:
- updated: float32 [864, 256, 512], P('comp', 'tile')
The draws below stay inside these ranges and needn't reach their ends.
Inputs may be any that keep to these rules, and one draw needn't show every extreme that they name: `sea_mask`: sea fractions vary from row to row and from tile to tile; a grid row may be wholly sea or wholly land.
All inputs are finite; a program needn't handle non-finite values.
Results may differ from the reference program's by a relative error of at most 0.00088.
Values sent between devices are 32-bit elements; how exact they have to be, the bound alone decides.
No kernel may reach another device: no remote copies, remote signals or barrier semaphores. Data moves between devices by JAX's collectives and lax.ppermute only.
A program may use at most 192 MiB of HBM per device.

```python
import math
import jax
import jax.numpy as jnp
from jax import lax

NTH = 36
NF = 24
NK = 864
NX = 512
NYT = 32
NY = 256


def draw_sea_mask(key, part):
    key = jax.random.fold_in(key, 11)
    key_tile, key_row, key_full, key_land, key_cell = jax.random.split(key, 5)
    tile_count = NY // NYT
    tile_level = jax.random.randint(key_tile, (tile_count,), 1, 5)
    row_level = jax.random.randint(key_row, (NY,), 1, 5)
    row_index = jnp.arange(NY, dtype=jnp.int32)
    level = jnp.minimum(row_level, tile_level[row_index // NYT])
    full_row = jax.random.randint(key_full, (), 0, NY)
    land_row = (full_row + jax.random.randint(key_land, (), 1, NY)) % NY
    level = jnp.where(row_index == full_row, 4, level)
    level = jnp.where(row_index == land_row, 0, level)
    cells = jax.random.randint(key_cell, (NY, NX), 0, 4)
    return (cells < level[:, None]).astype(jnp.int32)


def levels(own_key, shape, cuts, least, high):
    def one(axis_at, parts):
        steps = jax.random.uniform(jax.random.fold_in(jax.random.fold_in(own_key, 6), axis_at), (parts,), jnp.float32, least / len(cuts), high / len(cuts))
        return jnp.repeat(jnp.exp(steps), shape[axis_at] // parts).reshape((-1,) + (1,) * (len(shape) - axis_at - 1))

    factor_of = one(*cuts[0])
    for cut in cuts[1:]:
        factor_of = factor_of * one(*cut)
    return factor_of


def noise(key, extent, width, reach, shards=(), kind=jnp.bfloat16):
    values = jax.random.normal(key, extent, jnp.float32) * width
    if len(shards) > 0:
        values = levels(key, extent, shards, -0.22, 0.18) * values
    return jnp.clip(values, min=-reach, max=reach).astype(kind)


def setup_inputs(seed: int = 0) -> dict:
    key_of = jax.random.split(jax.random.key(seed), 11)
    return {
        "spectrum": jnp.clip(0.1 + 1.9 * jax.random.uniform(key_of[0], (NK, NY, NX), jnp.float32) ** levels(key_of[0], (NK, NY, NX), ((0, 32), (1, 8)), -0.2, 0.2), 0.1, 2.0),
        "speed": jnp.clip(jnp.exp(math.log(0.7) - 1.2527629 * jax.random.uniform(key_of[1], (NK,), jnp.float32) ** levels(key_of[1], (NK,), ((0, 32),), -0.2, 0.2)), 0.2, 0.7),
        "depth": jnp.clip(0.5 + 0.70000005 * jax.random.uniform(key_of[2], (NY, NX), jnp.float32) ** levels(key_of[2], (NY, NX), ((0, 8),), -0.2, 0.2), 0.5, 1.2),
        "turn": noise(key_of[3], (NY, NX), 1.0, 4.0, ((0, 8),), jnp.float32),
        "sea_mask": draw_sea_mask(jax.random.fold_in(key_of[10], 71), 0),
        "refraction": jnp.clip(jnp.exp(jax.random.uniform(key_of[5], (NF,), jnp.float32, math.log(0.1), math.log(0.6))), 0.1, 0.6),
        "growth": jnp.clip(jnp.exp(jax.random.uniform(key_of[6], (NK,), jnp.float32, math.log(0.1), math.log(1.0))), 0.1, 1.0),
        "dissipation": jnp.clip(jnp.exp(jax.random.uniform(key_of[7], (NK,), jnp.float32, math.log(0.1), math.log(1.0))), 0.1, 1.0),
        "quad_first": noise(key_of[8], (NK, NK), NK ** -0.5, 0.21875),
        "quad_second": noise(key_of[9], (NK, NK), NK ** -0.5, 0.21875),
    }


def third(padded, velocity, axis):
    count = padded.shape[axis] - 4
    back_two = lax.slice_in_dim(padded, 0, count, axis=axis)
    back_one = lax.slice_in_dim(padded, 1, count + 1, axis=axis)
    centre = lax.slice_in_dim(padded, 2, count + 2, axis=axis)
    ahead_one = lax.slice_in_dim(padded, 3, count + 3, axis=axis)
    ahead_two = lax.slice_in_dim(padded, 4, count + 4, axis=axis)
    positive = (2.0 * ahead_one + 3.0 * centre - 6.0 * back_one + back_two) / 6.0
    negative = (-ahead_two + 6.0 * ahead_one - 3.0 * centre - 2.0 * back_one) / 6.0
    return jnp.where(velocity >= 0.0, positive, negative)


def sources(flat, turn_flat, mask_flat, refraction, growth, dissipation, quad_first, quad_second):
    nfreq = refraction.shape[0]
    ncomp, npts = flat.shape
    grid = flat.reshape(nfreq, ncomp // nfreq, npts)
    rate = refraction[:, None, None] * turn_flat[None, None, :]
    ahead_one = jnp.roll(grid, -1, axis=1)
    ahead_two = jnp.roll(grid, -2, axis=1)
    back_one = jnp.roll(grid, 1, axis=1)
    back_two = jnp.roll(grid, 2, axis=1)
    positive = (2.0 * ahead_one + 3.0 * grid - 6.0 * back_one + back_two) / 6.0
    negative = (-ahead_two + 6.0 * ahead_one - 3.0 * grid - 2.0 * back_one) / 6.0
    turned = (grid - rate * jnp.where(rate >= 0.0, positive, negative)).reshape(ncomp, npts)
    low = turned.astype(jnp.bfloat16)
    partner = jnp.dot(quad_first, low, preferred_element_type=jnp.float32)
    pair = (turned * partner).astype(jnp.bfloat16)
    nonlinear = jnp.dot(quad_second, pair, preferred_element_type=jnp.float32)
    energy = jnp.mean(turned, axis=0)
    total = growth[:, None] * turned + nonlinear - dissipation[:, None] * turned * energy[None, :]
    return mask_flat[None, :] * (turned + 0.2 * total)


def reference(spectrum, speed, depth, turn, sea_mask, refraction, growth, dissipation, quad_first, quad_second):
    ncomp, nrows, ncols = spectrum.shape
    theta = (2.0 * math.pi / NTH) * jnp.arange(NTH).astype(jnp.float32)
    spec_four = spectrum.reshape(NF, NTH, nrows, ncols)
    speed_two = speed.reshape(NF, NTH)

    def propagate(freq):
        block = spec_four[freq]
        along = speed_two[freq]
        vel_x = along[:, None, None] * jnp.cos(theta)[:, None, None] * depth[None]
        vel_y = along[:, None, None] * jnp.sin(theta)[:, None, None] * depth[None]
        pad_x = jnp.pad(block, ((0, 0), (0, 0), (2, 2)))
        pad_y = jnp.pad(block, ((0, 0), (2, 2), (0, 0)))
        return block - vel_x * third(pad_x, vel_x, 2) - vel_y * third(pad_y, vel_y, 1)

    moved = lax.map(propagate, jnp.arange(NF).astype(jnp.int32)).reshape(ncomp, nrows, ncols)
    mask_float = sea_mask.astype(jnp.float32)
    nblocks = nrows // 8

    def update(index):
        first = (index * 8).astype(jnp.int32)
        rows = lax.dynamic_slice_in_dim(moved, first, 8, 1)
        turn_rows = lax.dynamic_slice_in_dim(turn, first, 8, 0)
        mask_rows = lax.dynamic_slice_in_dim(mask_float, first, 8, 0)
        result = sources(rows.reshape(ncomp, 8 * ncols), turn_rows.reshape(-1), mask_rows.reshape(-1),
                         refraction, growth, dissipation, quad_first, quad_second)
        return result.reshape(ncomp, 8, ncols)

    blocks = lax.map(update, jnp.arange(nblocks).astype(jnp.int32))
    return jnp.transpose(blocks, (1, 0, 2, 3)).reshape(ncomp, nrows, ncols)
```

```python
import functools
import math

import jax
import jax.numpy as jnp
from jax import lax
from jax.experimental import pallas as pl
from jax.experimental.pallas import tpu as pltpu
from jax.sharding import PartitionSpec as P

NTH = 36
HELD = 27
PAD = 32
ROWS = 32
COLS = 512
OWNERS = 32
LANES = 128
TILES = COLS // LANES
VMEM = pl.BlockSpec(memory_space=pltpu.VMEM)
SMEM = pl.BlockSpec(memory_space=pltpu.SMEM)
PARAMS = pltpu.CompilerParams(vmem_limit_bytes=24 * 2**20)


def iota(shape, dim):
    return lax.broadcasted_iota(jnp.int32, shape, dim)


def lane_gather(values, index):
    return jnp.take_along_axis(values, index, axis=1, mode="promise_in_bounds")


def wide(coef):
    return jnp.concatenate([coef] * TILES, axis=1)


def butterfly(rows, lane):
    for step, bit in ((1, 16), (2, 32), (4, 64)):
        swap = (lane & bit) != 0
        rows = [jnp.where(swap, rows[j ^ step], rows[j]) for j in range(8)]
    return rows


def mixed_plane(plane):
    lane = iota((ROWS, LANES), 1)
    row = iota((ROWS, LANES), 0)
    pieces = []
    for t in range(TILES):
        block = plane[:, t * LANES : (t + 1) * LANES]
        block = jnp.concatenate([block[(g ^ t) * 8 : (g ^ t) * 8 + 8] for g in range(4)], axis=0)
        for step, bit in ((1, 16), (2, 32), (4, 64)):
            swapped = jnp.where(
                (row & step) != 0,
                pltpu.roll(block, step, axis=0),
                pltpu.roll(block, ROWS - step, axis=0),
            )
            block = jnp.where((lane & bit) != 0, swapped, block)
        pieces.append(block)
    return jnp.concatenate(pieces, axis=1)


def propagate_kernel(
    spec, depth, turn, mask, speed, moved, halo_coef, pick, rank, turn_own, most, grid
):
    me = lax.axis_index("comp")
    sub = iota((PAD, LANES), 0)
    speeds = jnp.zeros((PAD, LANES), jnp.float32)
    for k in range(HELD):
        speeds = jnp.where(sub == k, speed[k], speeds)
    theta = (2.0 * math.pi / NTH) * lax.rem(me * HELD + sub, NTH).astype(jnp.float32)

    def taps(velocity):
        up = velocity >= 0.0
        sixth = velocity / 6.0
        return (
            sixth * jnp.where(up, 3.0, -3.0),
            sixth * jnp.where(up, 2.0, 6.0),
            sixth * jnp.where(up, -6.0, -2.0),
            jnp.where(up, sixth, 0.0),
            jnp.where(up, 0.0, -sixth),
        )

    x_centre, x_ahead, x_back, x_back_two, x_ahead_two = taps(speeds * jnp.cos(theta))
    y_centre, y_ahead, y_back, y_back_two, y_ahead_two = taps(speeds * jnp.sin(theta))
    halo_coef[0] = y_back
    halo_coef[1] = y_back_two
    halo_coef[2] = y_ahead
    halo_coef[3] = y_ahead_two

    for r in (0, 1, ROWS + 2, ROWS + 3):
        grid[r] = jnp.zeros((PAD, COLS), jnp.float32)
    for cb in range(4):
        size = min(8, HELD - cb * 8)
        for rb in range(4):
            block = spec[cb * 8 : cb * 8 + size, rb * 8 : rb * 8 + 8, :]
            if size < 8:
                block = jnp.concatenate(
                    [block, jnp.zeros((8 - size, 8, COLS), jnp.float32)], axis=0
                )
            grid[2 + rb * 8 : 10 + rb * 8, cb * 8 : cb * 8 + 8, :] = jnp.swapaxes(block, 0, 1)

    lane = iota((8, COLS), 1)
    for cb in range(4):
        part = slice(cb * 8, cb * 8 + 8)
        coefs = [
            wide(c[part])
            for c in (
                x_centre + y_centre, x_ahead, x_back, x_back_two, x_ahead_two,
                y_ahead, y_back, y_back_two, y_ahead_two,
            )
        ]

        def row_group(rb, carry):
            depths = depth[pl.ds(pl.multiple_of(rb * 8, 8), 8), :]
            for i in range(8):
                row_step(rb * 8 + i, depths[i : i + 1, :])
            return carry

        def row_step(r, depth_row):
            centre = grid[r + 2, part, :]
            total = coefs[0] * centre
            total += coefs[1] * jnp.where(lane < COLS - 1, pltpu.roll(centre, COLS - 1, axis=1), 0.0)
            total += coefs[2] * jnp.where(lane >= 1, pltpu.roll(centre, 1, axis=1), 0.0)
            total += coefs[3] * jnp.where(lane >= 2, pltpu.roll(centre, 2, axis=1), 0.0)
            total += coefs[4] * jnp.where(lane < COLS - 2, pltpu.roll(centre, COLS - 2, axis=1), 0.0)
            total += coefs[5] * grid[r + 3, part, :]
            total += coefs[6] * grid[r + 1, part, :]
            total += coefs[7] * grid[r, part, :]
            total += coefs[8] * grid[r + 4, part, :]
            moved[r, part, :] = centre - depth_row * total

        lax.fori_loop(0, ROWS // 8, row_group, 0)

    sea = mixed_plane(mask[...])
    column = iota((ROWS, COLS), 1)
    count = sea
    step = 1
    while step < COLS:
        count = count + jnp.where(column >= step, pltpu.roll(count, step, axis=1), 0)
        step *= 2
    most[0] = jnp.max(count)
    place = count - 1
    rank[...] = jnp.where(sea > 0, place, -1)
    entry = jnp.where(sea > 0, column * COLS + (column - place), -1)
    step = 1
    while step < COLS:
        other = pltpu.roll(entry, COLS - step, axis=1)
        arrives = (other >= 0) & ((other & step) != 0)
        stays = (entry >= 0) & ((entry & step) == 0)
        entry = jnp.where(arrives, other, jnp.where(stays, entry, -1))
        step *= 2
    entry = jnp.where(entry >= 0, entry >> 9, 0)
    pick[...] = entry

    mine = iota((ROWS, COLS), 0) == me
    own_turn = jnp.sum(jnp.where(mine, mixed_plane(turn[...]), 0.0), axis=0, keepdims=True)
    own_pick = jnp.sum(jnp.where(mine, entry, 0), axis=0, keepdims=True)
    for t in range(TILES):
        index = jnp.broadcast_to(own_pick[:, t * LANES : (t + 1) * LANES], (8, LANES))
        total = jnp.zeros((8, LANES), jnp.float32)
        for source in range(TILES):
            own = jnp.broadcast_to(own_turn[:, source * LANES : (source + 1) * LANES], (8, LANES))
            value = lane_gather(own, index & (LANES - 1))
            total = jnp.where(index >> 7 == source, value, total)
        turn_own[:, t * LANES : (t + 1) * LANES] = total


def propagate(spectrum, depth, turn, mask, speed):
    plane = jax.ShapeDtypeStruct((ROWS, COLS), jnp.int32)
    return pl.pallas_call(
        propagate_kernel,
        out_shape=[
            jax.ShapeDtypeStruct((ROWS, PAD, COLS), jnp.float32),
            jax.ShapeDtypeStruct((4, PAD, LANES), jnp.float32),
            plane,
            plane,
            jax.ShapeDtypeStruct((8, COLS), jnp.float32),
            jax.ShapeDtypeStruct((1,), jnp.int32),
        ],
        in_specs=[VMEM, VMEM, VMEM, VMEM, SMEM],
        out_specs=[VMEM, VMEM, VMEM, VMEM, VMEM, SMEM],
        scratch_shapes=[
            pltpu.VMEM((ROWS + 4, PAD, COLS), jnp.float32),
        ],
        compiler_params=PARAMS,
        cost_estimate=pl.CostEstimate(flops=20000000, bytes_accessed=5000000, transcendentals=0),
        name="propagate",
    )(spectrum, depth, turn, mask, speed)


def block_rows(tiles):
    return (HELD * tiles + 7) // 8 * 8


def compact_kernel(tiles, moved, low, high, depth, halo_coef, pick, out, mixed, edge):
    lane = iota((8, LANES), 1)
    back, back_two, ahead, ahead_two = [wide(halo_coef[i, 0:HELD, :]) for i in range(4)]
    terms = {
        0: back * low[1] + back_two * low[0],
        1: back_two * low[1],
        ROWS - 2: ahead_two * high[0],
        ROWS - 1: ahead * high[0] + ahead_two * high[1],
    }
    edge_of = {}
    for r, term in terms.items():
        edge_of[r] = len(edge_of)
        edge[edge_of[r], 0:HELD, :] = moved[r, 0:HELD, :] - depth[r : r + 1, :] * term

    def load(r, cb, t):
        rows, lanes = slice(cb * 8, cb * 8 + 8), slice(t * LANES, (t + 1) * LANES)
        return edge[edge_of[r], rows, lanes] if r in edge_of else moved[r, rows, lanes]

    for cb in range(4):
        for g in range(4):
            for t in range(TILES):
                rows = [load((g ^ t) * 8 + j, cb, t) for j in range(8)]
                for j, value in enumerate(butterfly(rows, lane)):
                    mixed[g * 8 + j, cb * 8 : cb * 8 + 8, t * LANES : (t + 1) * LANES] = value

    def owner_group(g, carry):
        picks = pick[pl.ds(pl.multiple_of(g * 8, 8), 8), :]
        for i in range(8):
            owner_step(g * 8 + i, picks[i : i + 1, :])
        return carry

    def owner_step(d, pick_row):
        for slot in range(tiles):
            index = jnp.broadcast_to(pick_row[:, slot * LANES : (slot + 1) * LANES], (8, LANES))
            tile_of = index >> 7
            index = index & (LANES - 1)
            for cb in range(4):
                total = lane_gather(
                    mixed[d, cb * 8 : cb * 8 + 8, slot * LANES : (slot + 1) * LANES], index
                )
                for source in range(slot + 1, TILES):
                    value = mixed[d, cb * 8 : cb * 8 + 8, source * LANES : (source + 1) * LANES]
                    total = jnp.where(tile_of == source, lane_gather(value, index), total)
                if cb < 3:
                    out[d, slot * 24 + cb * 8 : slot * 24 + cb * 8 + 8, :] = total
                else:
                    first = 24 * tiles + 3 * slot
                    out[d, first : first + 3, :] = total[0:3]

    lax.fori_loop(0, OWNERS // 8, owner_group, 0)


def compact(tiles, moved, low, high, depth, halo_coef, pick):
    return pl.pallas_call(
        functools.partial(compact_kernel, tiles),
        out_shape=jax.ShapeDtypeStruct((OWNERS, block_rows(tiles), LANES), jnp.float32),
        in_specs=[VMEM] * 6,
        out_specs=VMEM,
        scratch_shapes=[
            pltpu.VMEM((OWNERS, PAD, COLS), jnp.float32),
            pltpu.VMEM((4, PAD, COLS), jnp.float32),
        ],
        compiler_params=PARAMS,
        cost_estimate=pl.CostEstimate(flops=5000000, bytes_accessed=4000000, transcendentals=0),
        name="compact",
    )(moved, low, high, depth, halo_coef, pick)


def runs():
    found = []
    for s in range(OWNERS):
        k = 0
        while k < HELD:
            c = s * HELD + k
            end = min(24 if k < 24 else HELD, k + NTH - c % NTH)
            found.append((s, k, end - k, c))
            k = end
    return found


def block_row(tiles, slot, k):
    return slot * 24 + k if k < 24 else 24 * tiles + 3 * slot + k - 24


def source_kernel(
    tiles, points, turn_own, refraction, keep, lose, first, second, out, grid, turned, low, pair
):
    ncomp = turned.shape[0]
    nfreq = ncomp // NTH
    width = NTH + 4
    for slot in range(tiles):
        lanes = slice(slot * LANES, (slot + 1) * LANES)
        for s, k, size, c in runs():
            row = block_row(tiles, slot, k)
            to = c // NTH * width + 2 + c % NTH
            grid[to : to + size, lanes] = points[s, row : row + size, :]
        for f in range(nfreq):
            base = f * width
            grid[base : base + 2, lanes] = grid[base + NTH : base + NTH + 2, lanes]
            grid[base + NTH + 2 : base + NTH + 4, lanes] = grid[base + 2 : base + 4, lanes]
        for f in range(nfreq):
            base = f * width
            rate = refraction[f] * turn_own[0:1, lanes]
            up = rate >= 0.0
            sixth = rate / 6.0
            centre = grid[base : base + width, lanes]
            total = (sixth * jnp.where(up, 3.0, -3.0)) * centre
            total += (sixth * jnp.where(up, 2.0, 6.0)) * pltpu.roll(centre, width - 1, axis=0)
            total += (sixth * jnp.where(up, -6.0, -2.0)) * pltpu.roll(centre, 1, axis=0)
            total += jnp.where(up, sixth, 0.0) * pltpu.roll(centre, 2, axis=0)
            total += jnp.where(up, 0.0, -sixth) * pltpu.roll(centre, width - 2, axis=0)
            result = centre - total
            turned[f * NTH : (f + 1) * NTH, lanes] = result[2 : NTH + 2]

    chunk = ncomp // 3
    energy = jnp.zeros((1, tiles * LANES), jnp.float32)
    for m in range(0, ncomp, chunk):
        value = turned[m : m + chunk, :]
        low[m : m + chunk, :] = value.astype(jnp.bfloat16)
        energy += jnp.sum(value, axis=0, keepdims=True)
    energy = energy / ncomp
    for m in range(0, ncomp, chunk):
        partner = jnp.dot(
            first[m : m + chunk, :], low[...], preferred_element_type=jnp.float32
        )
        pair[m : m + chunk, :] = (turned[m : m + chunk, :] * partner).astype(jnp.bfloat16)
    for m in range(0, ncomp, chunk):
        nonlinear = jnp.dot(
            second[m : m + chunk, :], pair[...], preferred_element_type=jnp.float32
        )
        for slot in range(tiles):
            lanes = slice(slot * LANES, (slot + 1) * LANES)
            scale = keep[m : m + chunk, :] - lose[m : m + chunk, :] * energy[:, lanes]
            turned[m : m + chunk, lanes] = (
                turned[m : m + chunk, lanes] * scale + 0.2 * nonlinear[:, lanes]
            )
    for s in range(OWNERS):
        for slot in range(tiles):
            lanes = slice(slot * LANES, (slot + 1) * LANES)
            out[s, slot * 24 : slot * 24 + 24, :] = turned[s * HELD : s * HELD + 24, lanes]
            row = 24 * tiles + 3 * slot
            out[s, row : row + 3, :] = turned[s * HELD + 24 : s * HELD + HELD, lanes]


def sources(tiles, points, turn_own, refraction, keep, lose, first, second):
    ncomp = first.shape[0]
    lanes = tiles * LANES
    return pl.pallas_call(
        functools.partial(source_kernel, tiles),
        out_shape=jax.ShapeDtypeStruct(points.shape, jnp.float32),
        in_specs=[VMEM, VMEM, SMEM, VMEM, VMEM, VMEM, VMEM],
        out_specs=VMEM,
        scratch_shapes=[
            pltpu.VMEM((ncomp // NTH * (NTH + 4), lanes), jnp.float32),
            pltpu.VMEM((ncomp, lanes), jnp.float32),
            pltpu.VMEM((ncomp, lanes), jnp.bfloat16),
            pltpu.VMEM((ncomp, lanes), jnp.bfloat16),
        ],
        compiler_params=PARAMS,
        cost_estimate=pl.CostEstimate(
            flops=4 * ncomp * ncomp * lanes, bytes_accessed=6000000, transcendentals=0
        ),
        name="sources",
    )(points, turn_own, refraction, keep, lose, first, second)


def expand_kernel(tiles, result, rank, out, mixed):
    lane = iota((8, LANES), 1)

    def owner_group(g, carry):
        ranks = rank[pl.ds(pl.multiple_of(g * 8, 8), 8), :]
        for i in range(8):
            owner_step(g * 8 + i, ranks[i : i + 1, :])
        return carry

    def owner_step(d, rank_row):
        tail = result[d, 24 * tiles : 24 * tiles + 16, :]
        for t in range(TILES):
            index = jnp.broadcast_to(rank_row[:, t * LANES : (t + 1) * LANES], (8, LANES))
            slot_of = index >> 7
            land = index < 0
            index = index & (LANES - 1)
            for cb in range(4):
                total = jnp.zeros((8, LANES), jnp.float32)
                for slot in range(min(t + 1, tiles)):
                    if cb < 3:
                        row = slot * 24 + cb * 8
                        value = result[d, row : row + 8, :]
                    else:
                        value = pltpu.roll(tail, (16 - 3 * slot) % 16, axis=0)[0:8]
                    value = lane_gather(value, index)
                    total = value if slot == 0 else jnp.where(slot_of == slot, value, total)
                mixed[d, cb * 8 : cb * 8 + 8, t * LANES : (t + 1) * LANES] = jnp.where(
                    land, 0.0, total
                )

    lax.fori_loop(0, OWNERS // 8, owner_group, 0)
    for cb in range(4):
        size = min(8, HELD - cb * 8)
        for g in range(4):
            for t in range(TILES):
                rows = [
                    mixed[(g ^ t) * 8 + j, cb * 8 : cb * 8 + 8, t * LANES : (t + 1) * LANES]
                    for j in range(8)
                ]
                block = jnp.swapaxes(jnp.stack(butterfly(rows, lane)), 0, 1)
                out[cb * 8 : cb * 8 + size, g * 8 : g * 8 + 8, t * LANES : (t + 1) * LANES] = block[
                    0:size
                ]


def expand(tiles, result, rank):
    return pl.pallas_call(
        functools.partial(expand_kernel, tiles),
        out_shape=jax.ShapeDtypeStruct((HELD, ROWS, COLS), jnp.float32),
        in_specs=[VMEM] * 2,
        out_specs=VMEM,
        scratch_shapes=[pltpu.VMEM((OWNERS, PAD, COLS), jnp.float32)],
        compiler_params=PARAMS,
        cost_estimate=pl.CostEstimate(flops=5000000, bytes_accessed=4000000, transcendentals=0),
        name="expand",
    )(result, rank)


def exchange(blocks):
    return lax.all_to_all(blocks, "comp", split_axis=0, concat_axis=0, tiled=True)


def shards(
    spectrum, speed, depth, turn, sea_mask, refraction, growth, dissipation, quad_first, quad_second
):
    count = lax.axis_size("tile")
    forward = [(i, i + 1) for i in range(count - 1)]
    backward = [(i + 1, i) for i in range(count - 1)]
    low = lax.ppermute(jnp.swapaxes(spectrum[:, ROWS - 2 :, :], 0, 1), "tile", forward)
    high = lax.ppermute(jnp.swapaxes(spectrum[:, :2, :], 0, 1), "tile", backward)
    moved, halo_coef, pick, rank, turn_own, most = propagate(
        spectrum, depth, turn, sea_mask, speed
    )
    ncomp = growth.shape[0]
    keep = jnp.broadcast_to((1.0 + 0.2 * growth)[:, None], (ncomp, LANES))
    lose = jnp.broadcast_to((0.2 * dissipation)[:, None], (ncomp, LANES))

    def rest(tiles):
        def run(moved, low, high):
            sent = compact(tiles, moved, low, high, depth, halo_coef, pick)
            points = exchange(sent)
            result = sources(
                tiles, points, turn_own, refraction, keep, lose, quad_first, quad_second
            )
            return expand(tiles, exchange(result), rank)

        return run

    return lax.cond(most[0] <= 3 * LANES, rest(3), rest(4), moved, low, high)


def solution(mesh):
    in_specs = (
        P("comp", "tile", None),
        P("comp"),
        P("tile", None),
        P("tile", None),
        P("tile", None),
        P(),
        P(),
        P(),
        P(),
        P(),
    )
    out_specs = P("comp", "tile", None)
    return jax.shard_map(shards, mesh=mesh, in_specs=in_specs, out_specs=out_specs, check_vma=False)
```

```python
import functools
import math

import jax
import jax.numpy as jnp
from jax import lax
from jax.experimental import pallas as pl
from jax.experimental.pallas import tpu as pltpu
from jax.sharding import PartitionSpec as P

NTH = 36
HELD = 27
PAD = 32
ROWS = 32
COLS = 512
OWNERS = 32
LANES = 128
TILES = COLS // LANES
VMEM = pl.BlockSpec(memory_space=pltpu.VMEM)
SMEM = pl.BlockSpec(memory_space=pltpu.SMEM)
PARAMS = pltpu.CompilerParams(vmem_limit_bytes=24 * 2**20)


def iota(shape, dim):
    return lax.broadcasted_iota(jnp.int32, shape, dim)


def lane_gather(values, index):
    return jnp.take_along_axis(values, index, axis=1, mode="promise_in_bounds")


def wide(coef):
    return jnp.concatenate([coef] * TILES, axis=1)


def butterfly(rows, lane):
    for step, bit in ((1, 16), (2, 32), (4, 64)):
        swap = (lane & bit) != 0
        rows = [jnp.where(swap, rows[j ^ step], rows[j]) for j in range(8)]
    return rows


def mixed_plane(plane):
    lane = iota((ROWS, LANES), 1)
    row = iota((ROWS, LANES), 0)
    pieces = []
    for t in range(TILES):
        block = plane[:, t * LANES : (t + 1) * LANES]
        block = jnp.concatenate([block[(g ^ t) * 8 : (g ^ t) * 8 + 8] for g in range(4)], axis=0)
        for step, bit in ((1, 16), (2, 32), (4, 64)):
            swapped = jnp.where(
                (row & step) != 0,
                pltpu.roll(block, step, axis=0),
                pltpu.roll(block, ROWS - step, axis=0),
            )
            block = jnp.where((lane & bit) != 0, swapped, block)
        pieces.append(block)
    return jnp.concatenate(pieces, axis=1)


def prepare_kernel(
    spec, turn, mask, grid, low, high, pick, rank, turn_own, most, arrived, arriving
):
    copies = [
        pltpu.make_async_copy(
            spec.at[cb * 8 : min(cb * 8 + 8, HELD)],
            arrived.at[cb * 8 : min(cb * 8 + 8, HELD)],
            arriving.at[cb],
        )
        for cb in range(4)
    ]
    for copy in copies:
        copy.start()

    me = lax.axis_index("comp")
    sea = mixed_plane(mask[...])
    column = iota((ROWS, COLS), 1)
    count = sea
    step = 1
    while step < COLS:
        count = count + jnp.where(column >= step, pltpu.roll(count, step, axis=1), 0)
        step *= 2
    most[0] = jnp.max(count)
    place = count - 1
    rank[...] = jnp.where(sea > 0, place, -1)
    entry = jnp.where(sea > 0, column * COLS + (column - place), -1)
    step = 1
    while step < COLS:
        other = pltpu.roll(entry, COLS - step, axis=1)
        arrives = (other >= 0) & ((other & step) != 0)
        stays = (entry >= 0) & ((entry & step) == 0)
        entry = jnp.where(arrives, other, jnp.where(stays, entry, -1))
        step *= 2
    entry = jnp.where(entry >= 0, entry >> 9, 0)
    pick[...] = entry

    mine = iota((ROWS, COLS), 0) == me
    own_turn = jnp.sum(jnp.where(mine, mixed_plane(turn[...]), 0.0), axis=0, keepdims=True)
    own_pick = jnp.sum(jnp.where(mine, entry, 0), axis=0, keepdims=True)
    for t in range(TILES):
        index = jnp.broadcast_to(own_pick[:, t * LANES : (t + 1) * LANES], (8, LANES))
        total = jnp.zeros((8, LANES), jnp.float32)
        for source in range(TILES):
            own = jnp.broadcast_to(own_turn[:, source * LANES : (source + 1) * LANES], (8, LANES))
            value = lane_gather(own, index & (LANES - 1))
            total = jnp.where(index >> 7 == source, value, total)
        turn_own[:, t * LANES : (t + 1) * LANES] = total

    for cb in range(4):
        copies[cb].wait()
        part = slice(cb * 8, cb * 8 + 8)
        size = min(8, HELD - cb * 8)
        for rb in range(4):
            block = arrived[cb * 8 : cb * 8 + size, rb * 8 : rb * 8 + 8, :]
            if size < 8:
                block = jnp.concatenate(
                    [block, jnp.zeros((8 - size, 8, COLS), jnp.float32)], axis=0
                )
            block = jnp.swapaxes(block, 0, 1)
            grid[rb * 8 : rb * 8 + 8, part, :] = block
            if rb == 0:
                low[:, part, :] = block[0:2]
            if rb == 3:
                high[:, part, :] = block[6:8]


def prepare(spectrum, turn, mask):
    plane = jax.ShapeDtypeStruct((ROWS, COLS), jnp.int32)
    edge = jax.ShapeDtypeStruct((2, PAD, COLS), jnp.float32)
    return pl.pallas_call(
        prepare_kernel,
        out_shape=[
            jax.ShapeDtypeStruct((ROWS, PAD, COLS), jnp.float32),
            edge,
            edge,
            plane,
            plane,
            jax.ShapeDtypeStruct((8, COLS), jnp.float32),
            jax.ShapeDtypeStruct((1,), jnp.int32),
        ],
        in_specs=[pl.BlockSpec(memory_space=pl.ANY), VMEM, VMEM],
        out_specs=[VMEM] * 6 + [SMEM],
        scratch_shapes=[
            pltpu.VMEM((PAD, ROWS, COLS), jnp.float32),
            pltpu.SemaphoreType.DMA((4,)),
        ],
        compiler_params=PARAMS,
        cost_estimate=pl.CostEstimate(flops=2000000, bytes_accessed=4000000, transcendentals=0),
        name="prepare",
    )(spectrum, turn, mask)


def shifted(tiles, lane):
    ahead = [pltpu.roll(v, LANES - 1, axis=1) for v in tiles] + [0.0]
    back = [0.0] + [pltpu.roll(v, 1, axis=1) for v in tiles]
    ahead_two = [pltpu.roll(v, LANES - 2, axis=1) for v in tiles] + [0.0]
    back_two = [0.0] + [pltpu.roll(v, 2, axis=1) for v in tiles]
    return [
        (
            jnp.where(lane < LANES - 1, ahead[t], ahead[t + 1]),
            jnp.where(lane >= 1, back[t + 1], back[t]),
            jnp.where(lane < LANES - 2, ahead_two[t], ahead_two[t + 1]),
            jnp.where(lane >= 2, back_two[t + 1], back_two[t]),
        )
        for t in range(TILES)
    ]


def propagate_kernel(grid, depth, speed, moved, halo_coef):
    me = lax.axis_index("comp")
    sub = iota((PAD, LANES), 0)
    speeds = jnp.zeros((PAD, LANES), jnp.float32)
    for k in range(HELD):
        speeds = jnp.where(sub == k, speed[k], speeds)
    theta = (2.0 * math.pi / NTH) * lax.rem(me * HELD + sub, NTH).astype(jnp.float32)

    def taps(velocity):
        up = velocity >= 0.0
        sixth = velocity / 6.0
        return (
            sixth * jnp.where(up, 3.0, -3.0),
            sixth * jnp.where(up, 2.0, 6.0),
            sixth * jnp.where(up, -6.0, -2.0),
            jnp.where(up, sixth, -sixth),
            up,
        )

    x_centre, x_ahead, x_back, x_far, x_up = taps(speeds * jnp.cos(theta))
    y_centre, y_ahead, y_back, y_far, y_up = taps(speeds * jnp.sin(theta))
    halo_coef[0] = y_back
    halo_coef[1] = jnp.where(y_up, y_far, 0.0)
    halo_coef[2] = y_ahead
    halo_coef[3] = jnp.where(y_up, 0.0, y_far)
    centre_coef = x_centre + y_centre

    lane = iota((8, LANES), 1)
    for cb in range(4):
        part = slice(cb * 8, cb * 8 + 8)
        c0, xa, xb, xf, xu, ya, yb, yf, yu = [
            c[part]
            for c in (centre_coef, x_ahead, x_back, x_far, x_up, y_ahead, y_back, y_far, y_up)
        ]

        def row_step(r, rows, depth_row):
            centre = [grid[r, part, t * LANES : (t + 1) * LANES] for t in range(TILES)]

            def near(i, t):
                if not 0 <= rows + i < ROWS:
                    return jnp.zeros((8, LANES), jnp.float32)
                return grid[r + i, part, t * LANES : (t + 1) * LANES]

            for t, (ahead, back, ahead_two, back_two) in enumerate(shifted(centre, lane)):
                total = c0 * centre[t] + xa * ahead + xb * back
                total += xf * jnp.where(xu, back_two, ahead_two)
                total += ya * near(1, t) + yb * near(-1, t)
                total += yf * jnp.where(yu, near(-2, t), near(2, t))
                lanes = slice(t * LANES, (t + 1) * LANES)
                moved[r, part, lanes] = centre[t] - depth_row[:, lanes] * total

        def group(rb, first):
            depths = depth[pl.ds(pl.multiple_of(rb * 8, 8), 8), :]
            for i in range(8):
                row_step(rb * 8 + i, first + i, depths[i : i + 1, :])

        group(0, 0)

        @pl.loop(1, 3)
        def _(rb):
            group(rb, 8)

        group(3, 24)


def propagate(grid, depth, speed):
    return pl.pallas_call(
        propagate_kernel,
        out_shape=[
            jax.ShapeDtypeStruct((ROWS, PAD, COLS), jnp.float32),
            jax.ShapeDtypeStruct((4, PAD, LANES), jnp.float32),
        ],
        in_specs=[VMEM, VMEM, SMEM],
        out_specs=[VMEM, VMEM],
        compiler_params=PARAMS,
        cost_estimate=pl.CostEstimate(flops=20000000, bytes_accessed=4000000, transcendentals=0),
        name="propagate",
    )(grid, depth, speed)


def block_rows(tiles):
    return (HELD * tiles + 7) // 8 * 8


def compact_kernel(tiles, moved, low, high, depth, halo_coef, pick, out, mixed, edge):
    lane = iota((8, LANES), 1)
    back, back_two, ahead, ahead_two = [wide(halo_coef[i]) for i in range(4)]
    terms = {
        0: back * low[1] + back_two * low[0],
        1: back_two * low[1],
        ROWS - 2: ahead_two * high[0],
        ROWS - 1: ahead * high[0] + ahead_two * high[1],
    }
    edge_of = {}
    for r, term in terms.items():
        edge_of[r] = len(edge_of)
        edge[edge_of[r]] = moved[r] - depth[r : r + 1, :] * term

    def load(r, cb, t):
        rows, lanes = slice(cb * 8, cb * 8 + 8), slice(t * LANES, (t + 1) * LANES)
        return edge[edge_of[r], rows, lanes] if r in edge_of else moved[r, rows, lanes]

    for cb in range(4):
        for g in range(4):
            for t in range(TILES):
                rows = [load((g ^ t) * 8 + j, cb, t) for j in range(8)]
                for j, value in enumerate(butterfly(rows, lane)):
                    mixed[g * 8 + j, cb * 8 : cb * 8 + 8, t * LANES : (t + 1) * LANES] = value

    def owner_group(g, carry):
        picks = pick[pl.ds(pl.multiple_of(g * 8, 8), 8), :]
        for i in range(8):
            owner_step(g * 8 + i, picks[i : i + 1, :])
        return carry

    def owner_step(d, pick_row):
        for slot in range(tiles):
            index = jnp.broadcast_to(pick_row[:, slot * LANES : (slot + 1) * LANES], (8, LANES))
            tile_of = index >> 7
            index = index & (LANES - 1)
            for cb in range(4):
                total = lane_gather(
                    mixed[d, cb * 8 : cb * 8 + 8, slot * LANES : (slot + 1) * LANES], index
                )
                for source in range(slot + 1, TILES):
                    value = mixed[d, cb * 8 : cb * 8 + 8, source * LANES : (source + 1) * LANES]
                    total = jnp.where(tile_of == source, lane_gather(value, index), total)
                if cb < 3:
                    out[d, slot * 24 + cb * 8 : slot * 24 + cb * 8 + 8, :] = total
                else:
                    first = 24 * tiles + 3 * slot
                    out[d, first : first + 3, :] = total[0:3]

    lax.fori_loop(0, OWNERS // 8, owner_group, 0)


def compact(tiles, moved, low, high, depth, halo_coef, pick):
    return pl.pallas_call(
        functools.partial(compact_kernel, tiles),
        out_shape=jax.ShapeDtypeStruct((OWNERS, block_rows(tiles), LANES), jnp.float32),
        in_specs=[VMEM] * 6,
        out_specs=VMEM,
        scratch_shapes=[
            pltpu.VMEM((OWNERS, PAD, COLS), jnp.float32),
            pltpu.VMEM((4, PAD, COLS), jnp.float32),
        ],
        compiler_params=PARAMS,
        cost_estimate=pl.CostEstimate(flops=5000000, bytes_accessed=4000000, transcendentals=0),
        name="compact",
    )(moved, low, high, depth, halo_coef, pick)


def runs():
    found = []
    for s in range(OWNERS):
        k = 0
        while k < HELD:
            c = s * HELD + k
            end = min(24 if k < 24 else HELD, k + NTH - c % NTH)
            found.append((s, k, end - k, c))
            k = end
    return found


def block_row(tiles, slot, k):
    return slot * 24 + k if k < 24 else 24 * tiles + 3 * slot + k - 24


def source_kernel(
    tiles, points, turn_own, refraction, keep, lose, first, second, out, grid, turned, low, pair
):
    ncomp = turned.shape[0]
    nfreq = ncomp // NTH
    width = NTH + 4
    for slot in range(tiles):
        lanes = slice(slot * LANES, (slot + 1) * LANES)
        for s, k, size, c in runs():
            row = block_row(tiles, slot, k)
            to = c // NTH * width + 2 + c % NTH
            grid[to : to + size, lanes] = points[s, row : row + size, :]
        for f in range(nfreq):
            base = f * width
            grid[base : base + 2, lanes] = grid[base + NTH : base + NTH + 2, lanes]
            grid[base + NTH + 2 : base + NTH + 4, lanes] = grid[base + 2 : base + 4, lanes]
        for f in range(nfreq):
            base = f * width
            rate = refraction[f] * turn_own[0:1, lanes]
            up = rate >= 0.0
            sixth = rate / 6.0
            centre = grid[base : base + width, lanes]
            total = (sixth * jnp.where(up, 3.0, -3.0)) * centre
            total += (sixth * jnp.where(up, 2.0, 6.0)) * pltpu.roll(centre, width - 1, axis=0)
            total += (sixth * jnp.where(up, -6.0, -2.0)) * pltpu.roll(centre, 1, axis=0)
            total += jnp.where(up, sixth, 0.0) * pltpu.roll(centre, 2, axis=0)
            total += jnp.where(up, 0.0, -sixth) * pltpu.roll(centre, width - 2, axis=0)
            result = centre - total
            turned[f * NTH : (f + 1) * NTH, lanes] = result[2 : NTH + 2]

    chunk = ncomp // 3
    energy = jnp.zeros((1, tiles * LANES), jnp.float32)
    for m in range(0, ncomp, chunk):
        value = turned[m : m + chunk, :]
        low[m : m + chunk, :] = value.astype(jnp.bfloat16)
        energy += jnp.sum(value, axis=0, keepdims=True)
    energy = energy / ncomp
    for m in range(0, ncomp, chunk):
        partner = jnp.dot(
            first[m : m + chunk, :], low[...], preferred_element_type=jnp.float32
        )
        pair[m : m + chunk, :] = (turned[m : m + chunk, :] * partner).astype(jnp.bfloat16)
    for m in range(0, ncomp, chunk):
        nonlinear = jnp.dot(
            second[m : m + chunk, :], pair[...], preferred_element_type=jnp.float32
        )
        for slot in range(tiles):
            lanes = slice(slot * LANES, (slot + 1) * LANES)
            scale = keep[m : m + chunk, :] - lose[m : m + chunk, :] * energy[:, lanes]
            turned[m : m + chunk, lanes] = (
                turned[m : m + chunk, lanes] * scale + 0.2 * nonlinear[:, lanes]
            )
    for s in range(OWNERS):
        for slot in range(tiles):
            lanes = slice(slot * LANES, (slot + 1) * LANES)
            out[s, slot * 24 : slot * 24 + 24, :] = turned[s * HELD : s * HELD + 24, lanes]
            row = 24 * tiles + 3 * slot
            out[s, row : row + 3, :] = turned[s * HELD + 24 : s * HELD + HELD, lanes]


def sources(tiles, points, turn_own, refraction, keep, lose, first, second):
    ncomp = first.shape[0]
    lanes = tiles * LANES
    return pl.pallas_call(
        functools.partial(source_kernel, tiles),
        out_shape=jax.ShapeDtypeStruct(points.shape, jnp.float32),
        in_specs=[VMEM, VMEM, SMEM, VMEM, VMEM, VMEM, VMEM],
        out_specs=VMEM,
        scratch_shapes=[
            pltpu.VMEM((ncomp // NTH * (NTH + 4), lanes), jnp.float32),
            pltpu.VMEM((ncomp, lanes), jnp.float32),
            pltpu.VMEM((ncomp, lanes), jnp.bfloat16),
            pltpu.VMEM((ncomp, lanes), jnp.bfloat16),
        ],
        compiler_params=PARAMS,
        cost_estimate=pl.CostEstimate(
            flops=4 * ncomp * ncomp * lanes, bytes_accessed=6000000, transcendentals=0
        ),
        name="sources",
    )(points, turn_own, refraction, keep, lose, first, second)


def expand_kernel(tiles, result, rank, out, mixed):
    lane = iota((8, LANES), 1)

    def owner_group(g, carry):
        ranks = rank[pl.ds(pl.multiple_of(g * 8, 8), 8), :]
        for i in range(8):
            owner_step(g * 8 + i, ranks[i : i + 1, :])
        return carry

    def owner_step(d, rank_row):
        tail = result[d, 24 * tiles : 24 * tiles + 16, :]
        for t in range(TILES):
            index = jnp.broadcast_to(rank_row[:, t * LANES : (t + 1) * LANES], (8, LANES))
            slot_of = index >> 7
            land = index < 0
            index = index & (LANES - 1)
            for cb in range(4):
                total = jnp.zeros((8, LANES), jnp.float32)
                for slot in range(min(t + 1, tiles)):
                    if cb < 3:
                        row = slot * 24 + cb * 8
                        value = result[d, row : row + 8, :]
                    else:
                        value = pltpu.roll(tail, (16 - 3 * slot) % 16, axis=0)[0:8]
                    value = lane_gather(value, index)
                    total = value if slot == 0 else jnp.where(slot_of == slot, value, total)
                mixed[d, cb * 8 : cb * 8 + 8, t * LANES : (t + 1) * LANES] = jnp.where(
                    land, 0.0, total
                )

    lax.fori_loop(0, OWNERS // 8, owner_group, 0)
    for cb in range(4):
        size = min(8, HELD - cb * 8)
        for g in range(4):
            for t in range(TILES):
                rows = [
                    mixed[(g ^ t) * 8 + j, cb * 8 : cb * 8 + 8, t * LANES : (t + 1) * LANES]
                    for j in range(8)
                ]
                block = jnp.swapaxes(jnp.stack(butterfly(rows, lane)), 0, 1)
                out[cb * 8 : cb * 8 + size, g * 8 : g * 8 + 8, t * LANES : (t + 1) * LANES] = block[
                    0:size
                ]


def expand(tiles, result, rank):
    return pl.pallas_call(
        functools.partial(expand_kernel, tiles),
        out_shape=jax.ShapeDtypeStruct((HELD, ROWS, COLS), jnp.float32),
        in_specs=[VMEM] * 2,
        out_specs=VMEM,
        scratch_shapes=[pltpu.VMEM((OWNERS, PAD, COLS), jnp.float32)],
        compiler_params=PARAMS,
        cost_estimate=pl.CostEstimate(flops=5000000, bytes_accessed=4000000, transcendentals=0),
        name="expand",
    )(result, rank)


def exchange(blocks):
    return lax.all_to_all(blocks, "comp", split_axis=0, concat_axis=0, tiled=True)


def shards(
    spectrum, speed, depth, turn, sea_mask, refraction, growth, dissipation, quad_first, quad_second
):
    count = lax.axis_size("tile")
    forward = [(i, i + 1) for i in range(count - 1)]
    backward = [(i + 1, i) for i in range(count - 1)]
    grid, first, last, pick, rank, turn_own, most = prepare(spectrum, turn, sea_mask)
    low = lax.ppermute(last, "tile", forward)
    high = lax.ppermute(first, "tile", backward)
    moved, halo_coef = propagate(grid, depth, speed)
    ncomp = growth.shape[0]
    keep = jnp.broadcast_to((1.0 + 0.2 * growth)[:, None], (ncomp, LANES))
    lose = jnp.broadcast_to((0.2 * dissipation)[:, None], (ncomp, LANES))

    def rest(tiles):
        def run(moved, low, high):
            sent = compact(tiles, moved, low, high, depth, halo_coef, pick)
            points = exchange(sent)
            result = sources(
                tiles, points, turn_own, refraction, keep, lose, quad_first, quad_second
            )
            return expand(tiles, exchange(result), rank)

        return run

    return lax.cond(most[0] <= 3 * LANES, rest(3), rest(4), moved, low, high)


def solution(mesh):
    in_specs = (
        P("comp", "tile", None),
        P("comp"),
        P("tile", None),
        P("tile", None),
        P("tile", None),
        P(),
        P(),
        P(),
        P(),
        P(),
    )
    out_specs = P("comp", "tile", None)
    return jax.shard_map(shards, mesh=mesh, in_specs=in_specs, out_specs=out_specs, check_vma=False)
```

```python
import functools
import math

import jax
import jax.numpy as jnp
from jax import lax
from jax.experimental import pallas as pl
from jax.experimental.pallas import tpu as pltpu
from jax.sharding import PartitionSpec as P

NTH = 36
HELD = 27
PAD = 32
ROWS = 32
COLS = 512
OWNERS = 32
LANES = 128
TILES = COLS // LANES
VMEM = pl.BlockSpec(memory_space=pltpu.VMEM)
SMEM = pl.BlockSpec(memory_space=pltpu.SMEM)
ANY = pl.BlockSpec(memory_space=pl.ANY)
PARAMS = pltpu.CompilerParams(vmem_limit_bytes=24 * 2**20)


def iota(shape, dim):
    return lax.broadcasted_iota(jnp.int32, shape, dim)


def lane_gather(values, index):
    return jnp.take_along_axis(values, index, axis=1, mode="promise_in_bounds")


def wide(coef):
    return jnp.concatenate([coef] * TILES, axis=1)


def butterfly(rows, lane):
    for step, bit in ((1, 16), (2, 32), (4, 64)):
        swap = (lane & bit) != 0
        rows = [jnp.where(swap, rows[j ^ step], rows[j]) for j in range(8)]
    return rows


def mixed_plane(plane):
    lane = iota((ROWS, LANES), 1)
    row = iota((ROWS, LANES), 0)
    pieces = []
    for t in range(TILES):
        block = plane[:, t * LANES : (t + 1) * LANES]
        block = jnp.concatenate([block[(g ^ t) * 8 : (g ^ t) * 8 + 8] for g in range(4)], axis=0)
        for step, bit in ((1, 16), (2, 32), (4, 64)):
            swapped = jnp.where(
                (row & step) != 0,
                pltpu.roll(block, step, axis=0),
                pltpu.roll(block, ROWS - step, axis=0),
            )
            block = jnp.where((lane & bit) != 0, swapped, block)
        pieces.append(block)
    return jnp.concatenate(pieces, axis=1)


def prepare_kernel(spec, grid, low, high):
    for cb in range(4):
        part = slice(cb * 8, cb * 8 + 8)
        size = min(8, HELD - cb * 8)
        for rb in range(4):
            block = spec[cb * 8 : cb * 8 + size, rb * 8 : rb * 8 + 8, :]
            if size < 8:
                block = jnp.concatenate(
                    [block, jnp.zeros((8 - size, 8, COLS), jnp.float32)], axis=0
                )
            block = jnp.swapaxes(block, 0, 1)
            grid[rb * 8 : rb * 8 + 8, part, :] = block
            if rb == 0:
                low[:, part, :] = block[0:2]
            if rb == 3:
                high[:, part, :] = block[6:8]


def prepare(spectrum):
    edge = jax.ShapeDtypeStruct((2, PAD, COLS), jnp.float32)
    return pl.pallas_call(
        prepare_kernel,
        out_shape=[jax.ShapeDtypeStruct((ROWS, PAD, COLS), jnp.float32), edge, edge],
        in_specs=[VMEM],
        out_specs=[VMEM] * 3,
        compiler_params=PARAMS,
        cost_estimate=pl.CostEstimate(flops=2000000, bytes_accessed=4000000, transcendentals=0),
        name="prepare",
    )(spectrum)


def index_kernel(turn, mask, after, pick, rank, turn_own, most):
    me = lax.axis_index("comp")
    sea = mixed_plane(mask[...])
    column = iota((ROWS, COLS), 1)
    count = sea
    step = 1
    while step < COLS:
        count = count + jnp.where(column >= step, pltpu.roll(count, step, axis=1), 0)
        step *= 2
    most[0] = jnp.max(count)
    place = count - 1
    rank[...] = jnp.where(sea > 0, place, -1)
    entry = jnp.where(sea > 0, column * COLS + (column - place), -1)
    step = 1
    while step < COLS:
        other = pltpu.roll(entry, COLS - step, axis=1)
        arrives = (other >= 0) & ((other & step) != 0)
        stays = (entry >= 0) & ((entry & step) == 0)
        entry = jnp.where(arrives, other, jnp.where(stays, entry, -1))
        step *= 2
    entry = jnp.where(entry >= 0, entry >> 9, 0)
    pick[...] = entry

    mine = iota((ROWS, COLS), 0) == me
    own_turn = jnp.sum(jnp.where(mine, mixed_plane(turn[...]), 0.0), axis=0, keepdims=True)
    own_pick = jnp.sum(jnp.where(mine, entry, 0), axis=0, keepdims=True)
    for t in range(TILES):
        index = jnp.broadcast_to(own_pick[:, t * LANES : (t + 1) * LANES], (8, LANES))
        total = jnp.zeros((8, LANES), jnp.float32)
        for source in range(TILES):
            own = jnp.broadcast_to(own_turn[:, source * LANES : (source + 1) * LANES], (8, LANES))
            value = lane_gather(own, index & (LANES - 1))
            total = jnp.where(index >> 7 == source, value, total)
        turn_own[:, t * LANES : (t + 1) * LANES] = total


def make_index(turn, mask, after):
    plane = jax.ShapeDtypeStruct((ROWS, COLS), jnp.int32)
    return pl.pallas_call(
        index_kernel,
        out_shape=[
            plane,
            plane,
            jax.ShapeDtypeStruct((8, COLS), jnp.float32),
            jax.ShapeDtypeStruct((1,), jnp.int32),
        ],
        in_specs=[VMEM, VMEM, ANY],
        out_specs=[VMEM] * 3 + [SMEM],
        compiler_params=PARAMS,
        cost_estimate=pl.CostEstimate(flops=2000000, bytes_accessed=200000, transcendentals=0),
        name="index",
    )(turn, mask, after)


def shifted(tiles, lane):
    ahead = [pltpu.roll(v, LANES - 1, axis=1) for v in tiles] + [0.0]
    back = [0.0] + [pltpu.roll(v, 1, axis=1) for v in tiles]
    ahead_two = [pltpu.roll(v, LANES - 2, axis=1) for v in tiles] + [0.0]
    back_two = [0.0] + [pltpu.roll(v, 2, axis=1) for v in tiles]
    return [
        (
            jnp.where(lane < LANES - 1, ahead[t], ahead[t + 1]),
            jnp.where(lane >= 1, back[t + 1], back[t]),
            jnp.where(lane < LANES - 2, ahead_two[t], ahead_two[t + 1]),
            jnp.where(lane >= 2, back_two[t + 1], back_two[t]),
        )
        for t in range(TILES)
    ]


def propagate_kernel(grid, depth, speed, moved, halo_coef):
    me = lax.axis_index("comp")
    sub = iota((PAD, LANES), 0)
    speeds = jnp.zeros((PAD, LANES), jnp.float32)
    for k in range(HELD):
        speeds = jnp.where(sub == k, speed[k], speeds)
    theta = (2.0 * math.pi / NTH) * lax.rem(me * HELD + sub, NTH).astype(jnp.float32)

    def taps(velocity):
        up = velocity >= 0.0
        sixth = velocity / 6.0
        return (
            sixth * jnp.where(up, 3.0, -3.0),
            sixth * jnp.where(up, 2.0, 6.0),
            sixth * jnp.where(up, -6.0, -2.0),
            jnp.where(up, sixth, -sixth),
            up,
        )

    x_centre, x_ahead, x_back, x_far, x_up = taps(speeds * jnp.cos(theta))
    y_centre, y_ahead, y_back, y_far, y_up = taps(speeds * jnp.sin(theta))
    halo_coef[0] = y_back
    halo_coef[1] = jnp.where(y_up, y_far, 0.0)
    halo_coef[2] = y_ahead
    halo_coef[3] = jnp.where(y_up, 0.0, y_far)
    centre_coef = x_centre + y_centre

    lane = iota((8, LANES), 1)
    for cb in range(4):
        part = slice(cb * 8, cb * 8 + 8)
        c0, xa, xb, xf, xu, ya, yb, yf, yu = [
            c[part]
            for c in (centre_coef, x_ahead, x_back, x_far, x_up, y_ahead, y_back, y_far, y_up)
        ]

        def row_step(r, rows, depth_row):
            centre = [grid[r, part, t * LANES : (t + 1) * LANES] for t in range(TILES)]

            def near(i, t):
                if not 0 <= rows + i < ROWS:
                    return jnp.zeros((8, LANES), jnp.float32)
                return grid[r + i, part, t * LANES : (t + 1) * LANES]

            for t, (ahead, back, ahead_two, back_two) in enumerate(shifted(centre, lane)):
                total = c0 * centre[t] + xa * ahead + xb * back
                total += xf * jnp.where(xu, back_two, ahead_two)
                total += ya * near(1, t) + yb * near(-1, t)
                total += yf * jnp.where(yu, near(-2, t), near(2, t))
                lanes = slice(t * LANES, (t + 1) * LANES)
                moved[r, part, lanes] = centre[t] - depth_row[:, lanes] * total

        def group(rb, first):
            depths = depth[pl.ds(pl.multiple_of(rb * 8, 8), 8), :]
            for i in range(8):
                row_step(rb * 8 + i, first + i, depths[i : i + 1, :])

        group(0, 0)

        @pl.loop(1, 3)
        def _(rb):
            group(rb, 8)

        group(3, 24)


def propagate(grid, depth, speed):
    return pl.pallas_call(
        propagate_kernel,
        out_shape=[
            jax.ShapeDtypeStruct((ROWS, PAD, COLS), jnp.float32),
            jax.ShapeDtypeStruct((4, PAD, LANES), jnp.float32),
        ],
        in_specs=[VMEM, VMEM, SMEM],
        out_specs=[VMEM, VMEM],
        compiler_params=PARAMS,
        cost_estimate=pl.CostEstimate(flops=20000000, bytes_accessed=4000000, transcendentals=0),
        name="propagate",
    )(grid, depth, speed)


def block_rows(tiles):
    return (HELD * tiles + 7) // 8 * 8


def compact_kernel(tiles, moved, low, high, depth, halo_coef, pick, out, mixed, edge):
    lane = iota((8, LANES), 1)
    back, back_two, ahead, ahead_two = [wide(halo_coef[i]) for i in range(4)]
    terms = {
        0: back * low[1] + back_two * low[0],
        1: back_two * low[1],
        ROWS - 2: ahead_two * high[0],
        ROWS - 1: ahead * high[0] + ahead_two * high[1],
    }
    edge_of = {}
    for r, term in terms.items():
        edge_of[r] = len(edge_of)
        edge[edge_of[r]] = moved[r] - depth[r : r + 1, :] * term

    def load(r, cb, t):
        rows, lanes = slice(cb * 8, cb * 8 + 8), slice(t * LANES, (t + 1) * LANES)
        return edge[edge_of[r], rows, lanes] if r in edge_of else moved[r, rows, lanes]

    for cb in range(4):
        for g in range(4):
            for t in range(TILES):
                rows = [load((g ^ t) * 8 + j, cb, t) for j in range(8)]
                for j, value in enumerate(butterfly(rows, lane)):
                    mixed[g * 8 + j, cb * 8 : cb * 8 + 8, t * LANES : (t + 1) * LANES] = value

    def owner_group(g, carry):
        picks = pick[pl.ds(pl.multiple_of(g * 8, 8), 8), :]
        for i in range(8):
            owner_step(g * 8 + i, picks[i : i + 1, :])
        return carry

    def owner_step(d, pick_row):
        for slot in range(tiles):
            index = jnp.broadcast_to(pick_row[:, slot * LANES : (slot + 1) * LANES], (8, LANES))
            tile_of = index >> 7
            index = index & (LANES - 1)
            for cb in range(4):
                total = lane_gather(
                    mixed[d, cb * 8 : cb * 8 + 8, slot * LANES : (slot + 1) * LANES], index
                )
                for source in range(slot + 1, TILES):
                    value = mixed[d, cb * 8 : cb * 8 + 8, source * LANES : (source + 1) * LANES]
                    total = jnp.where(tile_of == source, lane_gather(value, index), total)
                if cb < 3:
                    out[d, slot * 24 + cb * 8 : slot * 24 + cb * 8 + 8, :] = total
                else:
                    first = 24 * tiles + 3 * slot
                    out[d, first : first + 3, :] = total[0:3]

    lax.fori_loop(0, OWNERS // 8, owner_group, 0)


def compact(tiles, moved, low, high, depth, halo_coef, pick):
    return pl.pallas_call(
        functools.partial(compact_kernel, tiles),
        out_shape=jax.ShapeDtypeStruct((OWNERS, block_rows(tiles), LANES), jnp.float32),
        in_specs=[VMEM] * 6,
        out_specs=VMEM,
        scratch_shapes=[
            pltpu.VMEM((OWNERS, PAD, COLS), jnp.float32),
            pltpu.VMEM((4, PAD, COLS), jnp.float32),
        ],
        compiler_params=PARAMS,
        cost_estimate=pl.CostEstimate(flops=5000000, bytes_accessed=4000000, transcendentals=0),
        name="compact",
    )(moved, low, high, depth, halo_coef, pick)


def runs():
    found = []
    for s in range(OWNERS):
        k = 0
        while k < HELD:
            c = s * HELD + k
            end = min(24 if k < 24 else HELD, k + NTH - c % NTH)
            found.append((s, k, end - k, c))
            k = end
    return found


def block_row(tiles, slot, k):
    return slot * 24 + k if k < 24 else 24 * tiles + 3 * slot + k - 24


def source_kernel(
    tiles, points, turn_own, refraction, keep, lose, first_far, second_far, out,
    grid, turned, low, pair, first, second, arriving,
):
    first_copy = pltpu.make_async_copy(first_far, first, arriving.at[0])
    first_copy.start()
    second_copy = pltpu.make_async_copy(second_far, second, arriving.at[1])
    second_copy.start()
    ncomp = turned.shape[0]
    nfreq = ncomp // NTH
    width = NTH + 4
    for slot in range(tiles):
        lanes = slice(slot * LANES, (slot + 1) * LANES)
        for s, k, size, c in runs():
            row = block_row(tiles, slot, k)
            to = c // NTH * width + 2 + c % NTH
            grid[to : to + size, lanes] = points[s, row : row + size, :]
        for f in range(nfreq):
            base = f * width
            grid[base : base + 2, lanes] = grid[base + NTH : base + NTH + 2, lanes]
            grid[base + NTH + 2 : base + NTH + 4, lanes] = grid[base + 2 : base + 4, lanes]
        for f in range(nfreq):
            base = f * width
            rate = refraction[f] * turn_own[0:1, lanes]
            up = rate >= 0.0
            sixth = rate / 6.0
            centre = grid[base : base + width, lanes]
            total = (sixth * jnp.where(up, 3.0, -3.0)) * centre
            total += (sixth * jnp.where(up, 2.0, 6.0)) * pltpu.roll(centre, width - 1, axis=0)
            total += (sixth * jnp.where(up, -6.0, -2.0)) * pltpu.roll(centre, 1, axis=0)
            total += jnp.where(up, sixth, 0.0) * pltpu.roll(centre, 2, axis=0)
            total += jnp.where(up, 0.0, -sixth) * pltpu.roll(centre, width - 2, axis=0)
            result = centre - total
            turned[f * NTH : (f + 1) * NTH, lanes] = result[2 : NTH + 2]

    chunk = ncomp // 3
    energy = jnp.zeros((1, tiles * LANES), jnp.float32)
    for m in range(0, ncomp, chunk):
        value = turned[m : m + chunk, :]
        low[m : m + chunk, :] = value.astype(jnp.bfloat16)
        energy += jnp.sum(value, axis=0, keepdims=True)
    energy = energy / ncomp
    first_copy.wait()
    partner = jnp.dot(first[...], low[...], preferred_element_type=jnp.float32)
    pair[...] = (turned[...] * partner).astype(jnp.bfloat16)
    second_copy.wait()
    nonlinear = jnp.dot(second[...], pair[...], preferred_element_type=jnp.float32)
    for slot in range(tiles):
        lanes = slice(slot * LANES, (slot + 1) * LANES)
        scale = keep[...] - lose[...] * energy[:, lanes]
        turned[:, lanes] = turned[:, lanes] * scale + 0.2 * nonlinear[:, lanes]
    for s in range(OWNERS):
        for slot in range(tiles):
            lanes = slice(slot * LANES, (slot + 1) * LANES)
            out[s, slot * 24 : slot * 24 + 24, :] = turned[s * HELD : s * HELD + 24, lanes]
            row = 24 * tiles + 3 * slot
            out[s, row : row + 3, :] = turned[s * HELD + 24 : s * HELD + HELD, lanes]


def sources(tiles, points, turn_own, refraction, keep, lose, first, second):
    ncomp = first.shape[0]
    lanes = tiles * LANES
    return pl.pallas_call(
        functools.partial(source_kernel, tiles),
        out_shape=jax.ShapeDtypeStruct(points.shape, jnp.float32),
        in_specs=[VMEM, VMEM, SMEM, VMEM, VMEM, ANY, ANY],
        out_specs=VMEM,
        scratch_shapes=[
            pltpu.VMEM((ncomp // NTH * (NTH + 4), lanes), jnp.float32),
            pltpu.VMEM((ncomp, lanes), jnp.float32),
            pltpu.VMEM((ncomp, lanes), jnp.bfloat16),
            pltpu.VMEM((ncomp, lanes), jnp.bfloat16),
            pltpu.VMEM((ncomp, ncomp), jnp.bfloat16),
            pltpu.VMEM((ncomp, ncomp), jnp.bfloat16),
            pltpu.SemaphoreType.DMA((2,)),
        ],
        compiler_params=PARAMS,
        cost_estimate=pl.CostEstimate(
            flops=4 * ncomp * ncomp * lanes, bytes_accessed=6000000, transcendentals=0
        ),
        name="sources",
    )(points, turn_own, refraction, keep, lose, first, second)


def expand_kernel(tiles, result, rank, mixed):
    def owner_group(g, carry):
        ranks = rank[pl.ds(pl.multiple_of(g * 8, 8), 8), :]
        for i in range(8):
            owner_step(g * 8 + i, ranks[i : i + 1, :])
        return carry

    def owner_step(d, rank_row):
        tail = result[d, 24 * tiles : 24 * tiles + 16, :]
        for t in range(TILES):
            index = jnp.broadcast_to(rank_row[:, t * LANES : (t + 1) * LANES], (8, LANES))
            slot_of = index >> 7
            land = index < 0
            index = index & (LANES - 1)
            for cb in range(4):
                total = jnp.zeros((8, LANES), jnp.float32)
                for slot in range(min(t + 1, tiles)):
                    if cb < 3:
                        row = slot * 24 + cb * 8
                        value = result[d, row : row + 8, :]
                    else:
                        value = pltpu.roll(tail, (16 - 3 * slot) % 16, axis=0)[0:8]
                    value = lane_gather(value, index)
                    total = value if slot == 0 else jnp.where(slot_of == slot, value, total)
                mixed[d, cb * 8 : cb * 8 + 8, t * LANES : (t + 1) * LANES] = jnp.where(
                    land, 0.0, total
                )

    lax.fori_loop(0, OWNERS // 8, owner_group, 0)


def expand(tiles, result, rank):
    return pl.pallas_call(
        functools.partial(expand_kernel, tiles),
        out_shape=jax.ShapeDtypeStruct((OWNERS, PAD, COLS), jnp.float32),
        in_specs=[VMEM] * 2,
        out_specs=VMEM,
        compiler_params=PARAMS,
        cost_estimate=pl.CostEstimate(flops=5000000, bytes_accessed=4000000, transcendentals=0),
        name="expand",
    )(result, rank)


def finish_kernel(mixed, out, done, leaving):
    lane = iota((8, LANES), 1)
    copies = []
    for cb in range(4):
        size = min(8, HELD - cb * 8)
        for g in range(4):
            for t in range(TILES):
                lanes = slice(t * LANES, (t + 1) * LANES)
                rows = [mixed[(g ^ t) * 8 + j, cb * 8 : cb * 8 + 8, lanes] for j in range(8)]
                block = jnp.swapaxes(jnp.stack(butterfly(rows, lane)), 0, 1)
                done[cb * 8 : cb * 8 + size, g * 8 : g * 8 + 8, lanes] = block[0:size]
        part = slice(cb * 8, cb * 8 + size)
        copies.append(pltpu.make_async_copy(done.at[part], out.at[part], leaving.at[cb]))
        copies[cb].start()
    for copy in copies:
        copy.wait()


def finish(mixed):
    return pl.pallas_call(
        finish_kernel,
        out_shape=jax.ShapeDtypeStruct((HELD, ROWS, COLS), jnp.float32),
        in_specs=[VMEM],
        out_specs=ANY,
        scratch_shapes=[
            pltpu.VMEM((HELD, ROWS, COLS), jnp.float32),
            pltpu.SemaphoreType.DMA((4,)),
        ],
        compiler_params=PARAMS,
        cost_estimate=pl.CostEstimate(flops=5000000, bytes_accessed=4000000, transcendentals=0),
        name="finish",
    )(mixed)


def exchange(blocks):
    return lax.all_to_all(blocks, "comp", split_axis=0, concat_axis=0, tiled=True)


def shards(
    spectrum, speed, depth, turn, sea_mask, refraction, growth, dissipation, quad_first, quad_second
):
    count = lax.axis_size("tile")
    forward = [(i, i + 1) for i in range(count - 1)]
    backward = [(i + 1, i) for i in range(count - 1)]
    grid, first, last = prepare(spectrum)
    low = lax.ppermute(last, "tile", forward)
    high = lax.ppermute(first, "tile", backward)
    moved, halo_coef = propagate(grid, depth, speed)
    pick, rank, turn_own, most = make_index(turn, sea_mask, halo_coef)
    ncomp = growth.shape[0]
    keep = jnp.broadcast_to((1.0 + 0.2 * growth)[:, None], (ncomp, LANES))
    lose = jnp.broadcast_to((0.2 * dissipation)[:, None], (ncomp, LANES))

    keep, lose = lax.optimization_barrier((keep, lose))

    def rest(tiles):
        def run(moved, low, high):
            sent = compact(tiles, moved, low, high, depth, halo_coef, pick)
            points = exchange(sent)
            result = sources(
                tiles, points, turn_own, refraction, keep, lose, quad_first, quad_second
            )
            return expand(tiles, exchange(result), rank)

        return run

    return finish(lax.cond(most[0] <= 3 * LANES, rest(3), rest(4), moved, low, high))


def solution(mesh):
    in_specs = (
        P("comp", "tile", None),
        P("comp"),
        P("tile", None),
        P("tile", None),
        P("tile", None),
        P(),
        P(),
        P(),
        P(),
        P(),
    )
    out_specs = P("comp", "tile", None)
    return jax.shard_map(shards, mesh=mesh, in_specs=in_specs, out_specs=out_specs, check_vma=False)
```

```python
import functools
import math

import jax
import jax.numpy as jnp
from jax import lax
from jax.experimental import pallas as pl
from jax.experimental.pallas import tpu as pltpu
from jax.sharding import PartitionSpec as P

NTH = 36
HELD = 27
PAD = 32
ROWS = 32
COLS = 512
OWNERS = 32
LANES = 128
TILES = COLS // LANES
VMEM = pl.BlockSpec(memory_space=pltpu.VMEM)
SMEM = pl.BlockSpec(memory_space=pltpu.SMEM)
ANY = pl.BlockSpec(memory_space=pl.ANY)
PARAMS = pltpu.CompilerParams(vmem_limit_bytes=24 * 2**20)


def iota(shape, dim):
    return lax.broadcasted_iota(jnp.int32, shape, dim)


def lane_gather(values, index):
    return jnp.take_along_axis(values, index, axis=1, mode="promise_in_bounds")


def wide(coef):
    return jnp.concatenate([coef] * TILES, axis=1)


def butterfly(rows, lane):
    for step, bit in ((1, 16), (2, 32), (4, 64)):
        swap = (lane & bit) != 0
        rows = [jnp.where(swap, rows[j ^ step], rows[j]) for j in range(8)]
    return rows


def mixed_plane(plane):
    lane = iota((ROWS, LANES), 1)
    row = iota((ROWS, LANES), 0)
    pieces = []
    for t in range(TILES):
        block = plane[:, t * LANES : (t + 1) * LANES]
        block = jnp.concatenate([block[(g ^ t) * 8 : (g ^ t) * 8 + 8] for g in range(4)], axis=0)
        for step, bit in ((1, 16), (2, 32), (4, 64)):
            swapped = jnp.where(
                (row & step) != 0,
                pltpu.roll(block, step, axis=0),
                pltpu.roll(block, ROWS - step, axis=0),
            )
            block = jnp.where((lane & bit) != 0, swapped, block)
        pieces.append(block)
    return jnp.concatenate(pieces, axis=1)


def prepare_kernel(spec, grid, low, high):
    for cb in range(4):
        part = slice(cb * 8, cb * 8 + 8)
        size = min(8, HELD - cb * 8)
        for rb in range(4):
            block = spec[cb * 8 : cb * 8 + size, rb * 8 : rb * 8 + 8, :]
            if size < 8:
                block = jnp.concatenate(
                    [block, jnp.zeros((8 - size, 8, COLS), jnp.float32)], axis=0
                )
            block = jnp.swapaxes(block, 0, 1)
            grid[rb * 8 : rb * 8 + 8, part, :] = block
            if rb == 0:
                low[:, part, :] = block[0:2]
            if rb == 3:
                high[:, part, :] = block[6:8]


def prepare(spectrum):
    edge = jax.ShapeDtypeStruct((2, PAD, COLS), jnp.float32)
    return pl.pallas_call(
        prepare_kernel,
        out_shape=[jax.ShapeDtypeStruct((ROWS, PAD, COLS), jnp.float32), edge, edge],
        in_specs=[VMEM],
        out_specs=[VMEM] * 3,
        compiler_params=PARAMS,
        cost_estimate=pl.CostEstimate(flops=2000000, bytes_accessed=4000000, transcendentals=0),
        name="prepare",
    )(spectrum)


def index_kernel(turn, mask, after, pick, rank, turn_own, most):
    me = lax.axis_index("comp")
    sea = mixed_plane(mask[...])
    column = iota((ROWS, COLS), 1)
    count = sea
    step = 1
    while step < COLS:
        count = count + jnp.where(column >= step, pltpu.roll(count, step, axis=1), 0)
        step *= 2
    most[0] = jnp.max(count)
    place = count - 1
    rank[...] = jnp.where(sea > 0, place, -1)
    entry = jnp.where(sea > 0, column * COLS + (column - place), -1)
    step = 1
    while step < COLS:
        other = pltpu.roll(entry, COLS - step, axis=1)
        arrives = (other >= 0) & ((other & step) != 0)
        stays = (entry >= 0) & ((entry & step) == 0)
        entry = jnp.where(arrives, other, jnp.where(stays, entry, -1))
        step *= 2
    entry = jnp.where(entry >= 0, entry >> 9, 0)
    pick[...] = entry

    mine = iota((ROWS, COLS), 0) == me
    own_turn = jnp.sum(jnp.where(mine, mixed_plane(turn[...]), 0.0), axis=0, keepdims=True)
    own_pick = jnp.sum(jnp.where(mine, entry, 0), axis=0, keepdims=True)
    for t in range(TILES):
        index = jnp.broadcast_to(own_pick[:, t * LANES : (t + 1) * LANES], (8, LANES))
        total = jnp.zeros((8, LANES), jnp.float32)
        for source in range(TILES):
            own = jnp.broadcast_to(own_turn[:, source * LANES : (source + 1) * LANES], (8, LANES))
            value = lane_gather(own, index & (LANES - 1))
            total = jnp.where(index >> 7 == source, value, total)
        turn_own[:, t * LANES : (t + 1) * LANES] = total


def make_index(turn, mask, after):
    plane = jax.ShapeDtypeStruct((ROWS, COLS), jnp.int32)
    return pl.pallas_call(
        index_kernel,
        out_shape=[
            plane,
            plane,
            jax.ShapeDtypeStruct((8, COLS), jnp.float32),
            jax.ShapeDtypeStruct((1,), jnp.int32),
        ],
        in_specs=[VMEM, VMEM, ANY],
        out_specs=[VMEM] * 3 + [SMEM],
        compiler_params=PARAMS,
        cost_estimate=pl.CostEstimate(flops=2000000, bytes_accessed=200000, transcendentals=0),
        name="index",
    )(turn, mask, after)


def shifted(tiles, lane):
    ahead = [pltpu.roll(v, LANES - 1, axis=1) for v in tiles] + [0.0]
    back = [0.0] + [pltpu.roll(v, 1, axis=1) for v in tiles]
    ahead_two = [pltpu.roll(v, LANES - 2, axis=1) for v in tiles] + [0.0]
    back_two = [0.0] + [pltpu.roll(v, 2, axis=1) for v in tiles]
    return [
        (
            jnp.where(lane < LANES - 1, ahead[t], ahead[t + 1]),
            jnp.where(lane >= 1, back[t + 1], back[t]),
            jnp.where(lane < LANES - 2, ahead_two[t], ahead_two[t + 1]),
            jnp.where(lane >= 2, back_two[t + 1], back_two[t]),
        )
        for t in range(TILES)
    ]


def propagate_kernel(grid, depth, speed, moved, halo_coef):
    me = lax.axis_index("comp")
    sub = iota((PAD, LANES), 0)
    speeds = jnp.zeros((PAD, LANES), jnp.float32)
    for k in range(HELD):
        speeds = jnp.where(sub == k, speed[k], speeds)
    theta = (2.0 * math.pi / NTH) * lax.rem(me * HELD + sub, NTH).astype(jnp.float32)

    def taps(velocity):
        up = velocity >= 0.0
        sixth = velocity / 6.0
        return (
            sixth * jnp.where(up, 3.0, -3.0),
            sixth * jnp.where(up, 2.0, 6.0),
            sixth * jnp.where(up, -6.0, -2.0),
            jnp.where(up, sixth, -sixth),
            up,
        )

    x_centre, x_ahead, x_back, x_far, x_up = taps(speeds * jnp.cos(theta))
    y_centre, y_ahead, y_back, y_far, y_up = taps(speeds * jnp.sin(theta))
    halo_coef[0] = y_back
    halo_coef[1] = jnp.where(y_up, y_far, 0.0)
    halo_coef[2] = y_ahead
    halo_coef[3] = jnp.where(y_up, 0.0, y_far)
    centre_coef = x_centre + y_centre

    lane = iota((8, LANES), 1)
    for cb in range(4):
        part = slice(cb * 8, cb * 8 + 8)
        c0, xa, xb, xf, xu, ya, yb, yf, yu = [
            c[part]
            for c in (centre_coef, x_ahead, x_back, x_far, x_up, y_ahead, y_back, y_far, y_up)
        ]

        def row_step(r, rows, depth_row):
            centre = [grid[r, part, t * LANES : (t + 1) * LANES] for t in range(TILES)]

            def near(i, t):
                if not 0 <= rows + i < ROWS:
                    return jnp.zeros((8, LANES), jnp.float32)
                return grid[r + i, part, t * LANES : (t + 1) * LANES]

            for t, (ahead, back, ahead_two, back_two) in enumerate(shifted(centre, lane)):
                total = c0 * centre[t] + xa * ahead + xb * back
                total += xf * jnp.where(xu, back_two, ahead_two)
                total += ya * near(1, t) + yb * near(-1, t)
                total += yf * jnp.where(yu, near(-2, t), near(2, t))
                lanes = slice(t * LANES, (t + 1) * LANES)
                moved[r, part, lanes] = centre[t] - depth_row[:, lanes] * total

        def group(rb, first):
            depths = depth[pl.ds(pl.multiple_of(rb * 8, 8), 8), :]
            for i in range(8):
                row_step(rb * 8 + i, first + i, depths[i : i + 1, :])

        group(0, 0)

        @pl.loop(1, 3)
        def _(rb):
            group(rb, 8)

        group(3, 24)


def propagate(grid, depth, speed):
    return pl.pallas_call(
        propagate_kernel,
        out_shape=[
            jax.ShapeDtypeStruct((ROWS, PAD, COLS), jnp.float32),
            jax.ShapeDtypeStruct((4, PAD, LANES), jnp.float32),
        ],
        in_specs=[VMEM, VMEM, SMEM],
        out_specs=[VMEM, VMEM],
        compiler_params=PARAMS,
        cost_estimate=pl.CostEstimate(flops=20000000, bytes_accessed=4000000, transcendentals=0),
        name="propagate",
    )(grid, depth, speed)


SHORT = 112
KINDS = ((2, SHORT), (3, 0), (4, 0))


def slots_of(kind):
    return kind[0] + (kind[1] > 0)


def block_rows(kind):
    return (24 * slots_of(kind) + 3 * kind[0] + 7) // 8 * 8


def tuck(row):
    spare = iota((8, LANES), 0) * 16 + (iota((8, LANES), 1) & 15)
    return lane_gather(jnp.broadcast_to(row, (8, LANES)), spare)


def untuck(rows):
    lane = iota((8, LANES), 1)
    value = lane_gather(rows, SHORT + (lane & 15))
    value = jnp.where(iota((8, LANES), 0) == lane >> 4, value, 0.0)
    for step in (4, 2, 1):
        value = value + pltpu.roll(value, step, axis=0)
    return value


def compact_kernel(kind, moved, low, high, depth, halo_coef, pick, out, mixed, edge):
    lane = iota((8, LANES), 1)
    back, back_two, ahead, ahead_two = [wide(halo_coef[i]) for i in range(4)]
    terms = {
        0: back * low[1] + back_two * low[0],
        1: back_two * low[1],
        ROWS - 2: ahead_two * high[0],
        ROWS - 1: ahead * high[0] + ahead_two * high[1],
    }
    edge_of = {}
    for r, term in terms.items():
        edge_of[r] = len(edge_of)
        edge[edge_of[r]] = moved[r] - depth[r : r + 1, :] * term

    def load(r, cb, t):
        rows, lanes = slice(cb * 8, cb * 8 + 8), slice(t * LANES, (t + 1) * LANES)
        return edge[edge_of[r], rows, lanes] if r in edge_of else moved[r, rows, lanes]

    for cb in range(4):
        for g in range(4):
            for t in range(TILES):
                rows = [load((g ^ t) * 8 + j, cb, t) for j in range(8)]
                for j, value in enumerate(butterfly(rows, lane)):
                    mixed[g * 8 + j, cb * 8 : cb * 8 + 8, t * LANES : (t + 1) * LANES] = value

    def owner_group(g, carry):
        picks = pick[pl.ds(pl.multiple_of(g * 8, 8), 8), :]
        for i in range(8):
            owner_step(g * 8 + i, picks[i : i + 1, :])
        return carry

    whole, short = kind

    def owner_step(d, pick_row):
        for slot in range(slots_of(kind)):
            index = jnp.broadcast_to(pick_row[:, slot * LANES : (slot + 1) * LANES], (8, LANES))
            tile_of = index >> 7
            index = index & (LANES - 1)
            values = []
            for cb in range(4):
                total = lane_gather(
                    mixed[d, cb * 8 : cb * 8 + 8, slot * LANES : (slot + 1) * LANES], index
                )
                for source in range(slot + 1, TILES):
                    value = mixed[d, cb * 8 : cb * 8 + 8, source * LANES : (source + 1) * LANES]
                    total = jnp.where(tile_of == source, lane_gather(value, index), total)
                values.append(total)
            for cb in range(3):
                value = values[cb]
                if slot >= whole:
                    value = jnp.where(lane < SHORT, value, tuck(values[3][cb : cb + 1]))
                out[d, slot * 24 + cb * 8 : slot * 24 + cb * 8 + 8, :] = value
            if slot < whole:
                row = 24 * slots_of(kind) + 3 * slot
                out[d, row : row + 3, :] = values[3][0:3]

    lax.fori_loop(0, OWNERS // 8, owner_group, 0)


def compact(kind, moved, low, high, depth, halo_coef, pick):
    return pl.pallas_call(
        functools.partial(compact_kernel, kind),
        out_shape=jax.ShapeDtypeStruct((OWNERS, block_rows(kind), LANES), jnp.float32),
        in_specs=[VMEM] * 6,
        out_specs=VMEM,
        scratch_shapes=[
            pltpu.VMEM((OWNERS, PAD, COLS), jnp.float32),
            pltpu.VMEM((4, PAD, COLS), jnp.float32),
        ],
        compiler_params=PARAMS,
        cost_estimate=pl.CostEstimate(flops=5000000, bytes_accessed=4000000, transcendentals=0),
        name="compact",
    )(moved, low, high, depth, halo_coef, pick)


def runs():
    found = []
    for s in range(OWNERS):
        k = 0
        while k < HELD:
            c = s * HELD + k
            end = min(24 if k < 24 else HELD, k + NTH - c % NTH)
            found.append((s, k, end - k, c))
            k = end
    return found


def columns(vector):
    pieces = []
    for begin in range(0, vector.shape[0], LANES):
        size = min(LANES, vector.shape[0] - begin)
        row = jnp.broadcast_to(vector[begin : begin + size][None, :], (8, size))
        if size < LANES:
            row = jnp.concatenate([row, jnp.zeros((8, LANES - size), jnp.float32)], axis=1)
        column = jnp.transpose(row)[:size, 0:1]
        pieces.append(jnp.broadcast_to(column, (size, LANES)))
    return pieces


def source_kernel(
    kind, points, turn_own, refraction, growth, dissipation, first_far, second_far, out,
    grid, turned, low, pair,
):
    first, second = first_far, second_far
    whole = kind[0]
    tiles = slots_of(kind)
    ncomp = low.shape[0]
    nfreq = ncomp // NTH
    width = NTH + 4
    for slot in range(tiles):
        lanes = slice(slot * LANES, (slot + 1) * LANES)
        for s, k, size, c in runs():
            to = c // NTH * width + 2 + c % NTH
            if k >= 24 and slot >= whole:
                for i in range(k - 24, k - 24 + size):
                    row = slot * 24 + i * 8
                    grid[slot, to : to + 1, :] = untuck(points[s, row : row + 8, :])[0:1]
                    to += 1
                continue
            row = slot * 24 + k if k < 24 else 24 * tiles + 3 * slot + k - 24
            grid[slot, to : to + size, :] = points[s, row : row + size, :]
        for f in range(nfreq):
            base = f * width
            grid[slot, base : base + 2, :] = grid[slot, base + NTH : base + NTH + 2, :]
            grid[slot, base + NTH + 2 : base + NTH + 4, :] = grid[slot, base + 2 : base + 4, :]
        turn_row = jnp.broadcast_to(turn_own[0:1, lanes], (8, LANES))
        up = turn_row >= 0.0
        sixth = turn_row / 6.0
        by_turn = [
            sixth * jnp.where(up, 3.0, -3.0),
            sixth * jnp.where(up, 2.0, 6.0),
            sixth * jnp.where(up, -6.0, -2.0),
            jnp.where(up, sixth, -sixth),
        ]
        for f in range(nfreq):
            base = f * width
            c0, ca, cb, cf = [c * refraction[f] for c in by_turn]
            for begin in range(0, NTH, 8):
                size = min(8, NTH - begin)
                at = base + 2 + begin

                def near(step):
                    return grid[slot, at + step : at + step + size, :]

                centre = near(0)
                total = c0[:size] * centre + ca[:size] * near(1) + cb[:size] * near(-1)
                total += cf[:size] * jnp.where(up[:size], near(-2), near(2))
                to = f * NTH + begin
                turned[slot, to : to + size, :] = centre - total

    energy = []
    for slot in range(tiles):
        value = turned[slot]
        low[:, slot * LANES : (slot + 1) * LANES] = value.astype(jnp.bfloat16)
        energy.append(jnp.sum(value, axis=0, keepdims=True) / ncomp)
    keep = [1.0 + 0.2 * column for column in columns(growth)]
    lose = [0.2 * column for column in columns(dissipation)]
    partner = jnp.dot(first[...], low[...], preferred_element_type=jnp.float32)
    for slot in range(tiles):
        lanes = slice(slot * LANES, (slot + 1) * LANES)
        pair[:, lanes] = (turned[slot] * partner[:, lanes]).astype(jnp.bfloat16)
    nonlinear = jnp.dot(second[...], pair[...], preferred_element_type=jnp.float32)
    for slot in range(tiles):
        lanes = slice(slot * LANES, (slot + 1) * LANES)
        for begin in range(0, ncomp, LANES):
            part = slice(begin, min(begin + LANES, ncomp))
            scale = keep[begin // LANES] - lose[begin // LANES] * energy[slot]
            turned[slot, part, :] = turned[slot, part, :] * scale + 0.2 * nonlinear[part, lanes]
    lane = iota((8, LANES), 1)
    for s in range(OWNERS):
        for slot in range(tiles):
            c = s * HELD
            if slot < whole:
                out[s, slot * 24 : slot * 24 + 24, :] = turned[slot, c : c + 24, :]
                row = 24 * tiles + 3 * slot
                out[s, row : row + 3, :] = turned[slot, c + 24 : c + HELD, :]
                continue
            for cb in range(3):
                value = turned[slot, c + cb * 8 : c + cb * 8 + 8, :]
                spare = tuck(turned[slot, c + 24 + cb : c + 25 + cb, :])
                row = slot * 24 + cb * 8
                out[s, row : row + 8, :] = jnp.where(lane < SHORT, value, spare)


def sources(kind, points, turn_own, refraction, growth, dissipation, first, second):
    ncomp = first.shape[0]
    tiles = slots_of(kind)
    lanes = tiles * LANES
    return pl.pallas_call(
        functools.partial(source_kernel, kind),
        out_shape=jax.ShapeDtypeStruct(points.shape, jnp.float32),
        in_specs=[VMEM, VMEM, SMEM, VMEM, VMEM, VMEM, VMEM],
        out_specs=VMEM,
        scratch_shapes=[
            pltpu.VMEM((tiles, ncomp // NTH * (NTH + 4), LANES), jnp.float32),
            pltpu.VMEM((tiles, ncomp, LANES), jnp.float32),
            pltpu.VMEM((ncomp, lanes), jnp.bfloat16),
            pltpu.VMEM((ncomp, lanes), jnp.bfloat16),
        ],
        compiler_params=PARAMS,
        cost_estimate=pl.CostEstimate(
            flops=4 * ncomp * ncomp * lanes, bytes_accessed=6000000, transcendentals=0
        ),
        name="sources",
    )(points, turn_own, refraction, growth, dissipation, first, second)


def expand_kernel(kind, result, rank, mixed):
    whole, short = kind
    slots = slots_of(kind)
    tail_rows = (3 * whole + 7) // 8 * 8
    row_at = iota((8, LANES), 0)

    def owner_group(g, carry):
        ranks = rank[pl.ds(pl.multiple_of(g * 8, 8), 8), :]
        for i in range(8):
            owner_step(g * 8 + i, ranks[i : i + 1, :])
        return carry

    def owner_step(d, rank_row):
        tail = result[d, 24 * slots : 24 * slots + tail_rows, :]
        values = []
        for slot in range(slots):
            parts = [result[d, slot * 24 + cb * 8 : slot * 24 + cb * 8 + 8, :] for cb in range(3)]
            if slot < whole:
                last = pltpu.roll(tail, (tail_rows - 3 * slot) % tail_rows, axis=0)[0:8]
            else:
                last = jnp.where(row_at == 1, untuck(parts[1]), untuck(parts[0]))
                last = jnp.where(row_at == 2, untuck(parts[2]), last)
            values.append(parts + [last])
        for t in range(TILES):
            index = jnp.broadcast_to(rank_row[:, t * LANES : (t + 1) * LANES], (8, LANES))
            slot_of = index >> 7
            land = index < 0
            index = index & (LANES - 1)
            for cb in range(4):
                total = lane_gather(values[0][cb], index)
                for slot in range(1, min(t + 1, slots)):
                    total = jnp.where(slot_of == slot, lane_gather(values[slot][cb], index), total)
                mixed[d, cb * 8 : cb * 8 + 8, t * LANES : (t + 1) * LANES] = jnp.where(
                    land, 0.0, total
                )

    lax.fori_loop(0, OWNERS // 8, owner_group, 0)


def expand(kind, result, rank):
    return pl.pallas_call(
        functools.partial(expand_kernel, kind),
        out_shape=jax.ShapeDtypeStruct((OWNERS, PAD, COLS), jnp.float32),
        in_specs=[VMEM] * 2,
        out_specs=VMEM,
        compiler_params=PARAMS,
        cost_estimate=pl.CostEstimate(flops=5000000, bytes_accessed=4000000, transcendentals=0),
        name="expand",
    )(result, rank)


def finish_kernel(mixed, out, done, leaving):
    lane = iota((8, LANES), 1)
    copies = []
    for cb in range(4):
        size = min(8, HELD - cb * 8)
        for g in range(4):
            for t in range(TILES):
                lanes = slice(t * LANES, (t + 1) * LANES)
                rows = [mixed[(g ^ t) * 8 + j, cb * 8 : cb * 8 + 8, lanes] for j in range(8)]
                block = jnp.swapaxes(jnp.stack(butterfly(rows, lane)), 0, 1)
                done[cb * 8 : cb * 8 + size, g * 8 : g * 8 + 8, lanes] = block[0:size]
        part = slice(cb * 8, cb * 8 + size)
        copies.append(pltpu.make_async_copy(done.at[part], out.at[part], leaving.at[cb]))
        copies[cb].start()
    for copy in copies:
        copy.wait()


def finish(mixed):
    return pl.pallas_call(
        finish_kernel,
        out_shape=jax.ShapeDtypeStruct((HELD, ROWS, COLS), jnp.float32),
        in_specs=[VMEM],
        out_specs=ANY,
        scratch_shapes=[
            pltpu.VMEM((HELD, ROWS, COLS), jnp.float32),
            pltpu.SemaphoreType.DMA((4,)),
        ],
        compiler_params=PARAMS,
        cost_estimate=pl.CostEstimate(flops=5000000, bytes_accessed=4000000, transcendentals=0),
        name="finish",
    )(mixed)


def exchange(blocks):
    return lax.all_to_all(blocks, "comp", split_axis=0, concat_axis=0, tiled=True)


def shards(
    spectrum, speed, depth, turn, sea_mask, refraction, growth, dissipation, quad_first, quad_second
):
    count = lax.axis_size("tile")
    forward = [(i, i + 1) for i in range(count - 1)]
    backward = [(i + 1, i) for i in range(count - 1)]
    grid, first, last = prepare(spectrum)
    low = lax.ppermute(last, "tile", forward)
    high = lax.ppermute(first, "tile", backward)
    moved, halo_coef = propagate(grid, depth, speed)
    pick, rank, turn_own, most = make_index(turn, sea_mask, halo_coef)

    def rest(kind):
        def run(moved, low, high):
            sent = compact(kind, moved, low, high, depth, halo_coef, pick)
            points = exchange(sent)
            result = sources(
                kind, points, turn_own, refraction, growth, dissipation, quad_first, quad_second
            )
            return expand(kind, exchange(result), rank)

        return run

    limits = [whole * LANES + short for whole, short in KINDS[:-1]]
    chosen = sum((most[0] > limit).astype(jnp.int32) for limit in limits)
    return finish(lax.switch(chosen, [rest(kind) for kind in KINDS], moved, low, high))


def solution(mesh):
    in_specs = (
        P("comp", "tile", None),
        P("comp"),
        P("tile", None),
        P("tile", None),
        P("tile", None),
        P(),
        P(),
        P(),
        P(),
        P(),
    )
    out_specs = P("comp", "tile", None)
    return jax.shard_map(shards, mesh=mesh, in_specs=in_specs, out_specs=out_specs, check_vma=False)
```

```python
import functools
import math

import jax
import jax.numpy as jnp
from jax import lax
from jax.experimental import pallas as pl
from jax.experimental.pallas import tpu as pltpu
from jax.sharding import PartitionSpec as P

NTH = 36
HELD = 27
PAD = 32
ROWS = 32
COLS = 512
OWNERS = 32
LANES = 128
TILES = COLS // LANES
VMEM = pl.BlockSpec(memory_space=pltpu.VMEM)
SMEM = pl.BlockSpec(memory_space=pltpu.SMEM)
ANY = pl.BlockSpec(memory_space=pl.ANY)
PARAMS = pltpu.CompilerParams(vmem_limit_bytes=24 * 2**20)


def iota(shape, dim):
    return lax.broadcasted_iota(jnp.int32, shape, dim)


def lane_gather(values, index):
    return jnp.take_along_axis(values, index, axis=1, mode="promise_in_bounds")


def wide(coef):
    return jnp.concatenate([coef] * TILES, axis=1)


def butterfly(rows, lane):
    for step, bit in ((1, 16), (2, 32), (4, 64)):
        swap = (lane & bit) != 0
        rows = [jnp.where(swap, rows[j ^ step], rows[j]) for j in range(8)]
    return rows


def mixed_plane(plane):
    lane = iota((ROWS, LANES), 1)
    row = iota((ROWS, LANES), 0)
    pieces = []
    for t in range(TILES):
        block = plane[:, t * LANES : (t + 1) * LANES]
        block = jnp.concatenate([block[(g ^ t) * 8 : (g ^ t) * 8 + 8] for g in range(4)], axis=0)
        for step, bit in ((1, 16), (2, 32), (4, 64)):
            swapped = jnp.where(
                (row & step) != 0,
                pltpu.roll(block, step, axis=0),
                pltpu.roll(block, ROWS - step, axis=0),
            )
            block = jnp.where((lane & bit) != 0, swapped, block)
        pieces.append(block)
    return jnp.concatenate(pieces, axis=1)


def prepare_kernel(spec, grid, low, high):
    for cb in range(4):
        part = slice(cb * 8, cb * 8 + 8)
        size = min(8, HELD - cb * 8)
        for rb in range(4):
            block = spec[cb * 8 : cb * 8 + size, rb * 8 : rb * 8 + 8, :]
            if size < 8:
                block = jnp.concatenate(
                    [block, jnp.zeros((8 - size, 8, COLS), jnp.float32)], axis=0
                )
            block = jnp.swapaxes(block, 0, 1)
            grid[rb * 8 : rb * 8 + 8, part, :] = block
            if rb == 0:
                low[:, part, :] = block[0:2]
            if rb == 3:
                high[:, part, :] = block[6:8]


def prepare(spectrum):
    edge = jax.ShapeDtypeStruct((2, PAD, COLS), jnp.float32)
    return pl.pallas_call(
        prepare_kernel,
        out_shape=[jax.ShapeDtypeStruct((ROWS, PAD, COLS), jnp.float32), edge, edge],
        in_specs=[VMEM],
        out_specs=[VMEM] * 3,
        compiler_params=PARAMS,
        cost_estimate=pl.CostEstimate(flops=2000000, bytes_accessed=4000000, transcendentals=0),
        name="prepare",
    )(spectrum)


def index_steps(me, turn, mask, pick, rank, turn_own, chosen):
    sea = mixed_plane(mask[...])
    yield
    column = iota((ROWS, COLS), 1)
    count = sea
    step = 1
    while step < COLS:
        count = count + jnp.where(column >= step, pltpu.roll(count, step, axis=1), 0)
        step *= 2
        if step <= LANES:
            yield
    largest = jnp.max(count)
    kind = jnp.int32(0)
    for whole, short in KINDS[:-1]:
        kind += (largest > whole * LANES + short).astype(jnp.int32)
    chosen[0] = kind
    place = count - 1
    rank[...] = jnp.where(sea > 0, place, -1)
    entry = jnp.where(sea > 0, column * COLS + (column - place), -1)
    step = 1
    while step < COLS:
        other = pltpu.roll(entry, COLS - step, axis=1)
        arrives = (other >= 0) & ((other & step) != 0)
        stays = (entry >= 0) & ((entry & step) == 0)
        entry = jnp.where(arrives, other, jnp.where(stays, entry, -1))
        step *= 2
        if step <= LANES:
            yield
    entry = jnp.where(entry >= 0, entry >> 9, 0)
    pick[...] = entry
    mine = iota((ROWS, COLS), 0) == me
    own_turn = jnp.sum(jnp.where(mine, mixed_plane(turn[...]), 0.0), axis=0, keepdims=True)
    own_pick = jnp.sum(jnp.where(mine, entry, 0), axis=0, keepdims=True)
    for t in range(TILES):
        index = jnp.broadcast_to(own_pick[:, t * LANES : (t + 1) * LANES], (8, LANES))
        total = jnp.zeros((8, LANES), jnp.float32)
        for source in range(TILES):
            own = jnp.broadcast_to(own_turn[:, source * LANES : (source + 1) * LANES], (8, LANES))
            value = lane_gather(own, index & (LANES - 1))
            total = jnp.where(index >> 7 == source, value, total)
        turn_own[:, t * LANES : (t + 1) * LANES] = total
    yield


def shifted(tiles, lane):
    ahead = [pltpu.roll(v, LANES - 1, axis=1) for v in tiles] + [0.0]
    back = [0.0] + [pltpu.roll(v, 1, axis=1) for v in tiles]
    ahead_two = [pltpu.roll(v, LANES - 2, axis=1) for v in tiles] + [0.0]
    back_two = [0.0] + [pltpu.roll(v, 2, axis=1) for v in tiles]
    return [
        (
            jnp.where(lane < LANES - 1, ahead[t], ahead[t + 1]),
            jnp.where(lane >= 1, back[t + 1], back[t]),
            jnp.where(lane < LANES - 2, ahead_two[t], ahead_two[t + 1]),
            jnp.where(lane >= 2, back_two[t + 1], back_two[t]),
        )
        for t in range(TILES)
    ]


def propagate_kernel(
    grid, depth, turn, mask, speed, mixed, halo_coef, pick, rank, turn_own, chosen
):
    me = lax.axis_index("comp")
    beside = index_steps(me, turn, mask, pick, rank, turn_own, chosen)
    sub = iota((PAD, LANES), 0)
    speeds = jnp.zeros((PAD, LANES), jnp.float32)
    for k in range(HELD):
        speeds = jnp.where(sub == k, speed[k], speeds)
    theta = (2.0 * math.pi / NTH) * lax.rem(me * HELD + sub, NTH).astype(jnp.float32)

    def taps(velocity):
        up = velocity >= 0.0
        sixth = velocity / 6.0
        return (
            sixth * jnp.where(up, 3.0, -3.0),
            sixth * jnp.where(up, 2.0, 6.0),
            sixth * jnp.where(up, -6.0, -2.0),
            jnp.where(up, sixth, -sixth),
            up,
        )

    x_centre, x_ahead, x_back, x_far, x_up = taps(speeds * jnp.cos(theta))
    y_centre, y_ahead, y_back, y_far, y_up = taps(speeds * jnp.sin(theta))
    halo_coef[0] = y_back
    halo_coef[1] = jnp.where(y_up, y_far, 0.0)
    halo_coef[2] = y_ahead
    halo_coef[3] = jnp.where(y_up, 0.0, y_far)
    centre_coef = x_centre + y_centre

    lane = iota((8, LANES), 1)
    for cb in range(4):
        part = slice(cb * 8, cb * 8 + 8)
        c0, xa, xb, xf, xu, ya, yb, yf, yu = [
            c[part]
            for c in (centre_coef, x_ahead, x_back, x_far, x_up, y_ahead, y_back, y_far, y_up)
        ]

        def row_step(r, rows, depth_row):
            results = []
            centre = [grid[r, part, t * LANES : (t + 1) * LANES] for t in range(TILES)]

            def near(i, t):
                if not 0 <= rows + i < ROWS:
                    return jnp.zeros((8, LANES), jnp.float32)
                return grid[r + i, part, t * LANES : (t + 1) * LANES]

            for t, (ahead, back, ahead_two, back_two) in enumerate(shifted(centre, lane)):
                total = c0 * centre[t] + xa * ahead + xb * back
                total += xf * jnp.where(xu, back_two, ahead_two)
                total += ya * near(1, t) + yb * near(-1, t)
                total += yf * jnp.where(yu, near(-2, t), near(2, t))
                lanes = slice(t * LANES, (t + 1) * LANES)
                results.append(centre[t] - depth_row[:, lanes] * total)
            return results

        for rb in range(ROWS // 8):
            depths = depth[rb * 8 : rb * 8 + 8, :]
            group = [row_step(rb * 8 + i, rb * 8 + i, depths[i : i + 1, :]) for i in range(8)]
            for t in range(TILES):
                for j, value in enumerate(butterfly([row[t] for row in group], lane)):
                    mixed[(rb ^ t) * 8 + j, part, t * LANES : (t + 1) * LANES] = value
            next(beside, None)
    for _ in beside:
        pass


def propagate(grid, depth, turn, mask, speed):
    plane = jax.ShapeDtypeStruct((ROWS, COLS), jnp.int32)
    return pl.pallas_call(
        propagate_kernel,
        out_shape=[
            jax.ShapeDtypeStruct((ROWS, PAD, COLS), jnp.float32),
            jax.ShapeDtypeStruct((4, PAD, LANES), jnp.float32),
            plane,
            plane,
            jax.ShapeDtypeStruct((8, COLS), jnp.float32),
            jax.ShapeDtypeStruct((1,), jnp.int32),
        ],
        in_specs=[VMEM, VMEM, VMEM, VMEM, SMEM],
        out_specs=[VMEM] * 5 + [SMEM],
        compiler_params=PARAMS,
        cost_estimate=pl.CostEstimate(flops=20000000, bytes_accessed=4000000, transcendentals=0),
        name="propagate",
    )(grid, depth, turn, mask, speed)


SHORT = 112
KINDS = ((2, SHORT), (3, 0), (4, 0))


def slots_of(kind):
    return kind[0] + (kind[1] > 0)


def block_rows(kind):
    return (24 * slots_of(kind) + 3 * kind[0] + 7) // 8 * 8


def tuck(row):
    spare = iota((8, LANES), 0) * 16 + (iota((8, LANES), 1) & 15)
    return lane_gather(jnp.broadcast_to(row, (8, LANES)), spare)


def untuck(rows):
    lane = iota((8, LANES), 1)
    value = lane_gather(rows, SHORT + (lane & 15))
    value = jnp.where(iota((8, LANES), 0) == lane >> 4, value, 0.0)
    for step in (4, 2, 1):
        value = value + pltpu.roll(value, step, axis=0)
    return value


def compact_kernel(kind, mixed, low, high, depth, halo_coef, pick, out, terms, fixed, spare, tails):
    lane = iota((8, LANES), 1)
    strip = lane >> 4
    back, back_two, ahead, ahead_two = [wide(halo_coef[i]) for i in range(4)]
    terms[0] = depth[0:1, :] * (back * low[1] + back_two * low[0])
    terms[1] = depth[1:2, :] * (back_two * low[1])
    terms[2] = depth[ROWS - 2 : ROWS - 1, :] * (ahead_two * high[0])
    terms[3] = depth[ROWS - 1 : ROWS, :] * (ahead * high[0] + ahead_two * high[1])

    for g in range(4):
        for first, row, t in ((0, 0, g), (2, 6, 3 - g)):
            lanes = slice(t * LANES, (t + 1) * LANES)
            for cb in range(4):
                part = slice(cb * 8, cb * 8 + 8)
                one, two = terms[first, part, lanes], terms[first + 1, part, lanes]
                for j in range(8):
                    term = jnp.where(strip == (row + 1) ^ j, two, 0.0)
                    term = jnp.where(strip == row ^ j, one, term)
                    fixed[g * 8 + j, first // 2, part, :] = mixed[g * 8 + j, part, lanes] - term

    whole, short = kind

    def load(d, cb, t):
        part = slice(cb * 8, cb * 8 + 8)
        if t == d // 8:
            return fixed[d, 0, part, :]
        if t == 3 - d // 8:
            return fixed[d, 1, part, :]
        return mixed[d, part, t * LANES : (t + 1) * LANES]

    def index_of(d, slot):
        index = jnp.broadcast_to(pick[d : d + 1, slot * LANES : (slot + 1) * LANES], (8, LANES))
        return index & (LANES - 1), [index >> 7 == t for t in range(TILES)]

    def picked(d, cb, slot, index, among):
        total = lane_gather(load(d, cb, slot), index)
        for source in range(slot + 1, TILES):
            value = lane_gather(load(d, cb, source), index)
            total = jnp.where(among[source], value, total)
        return total

    if short:
        for d in range(OWNERS):
            tails[d] = picked(d, 3, whole, *index_of(d, whole))
        for d in range(OWNERS):
            for cb in range(3):
                spare[d, cb] = tuck(tails[d, cb : cb + 1, :])

    for d in range(OWNERS):
        for slot in range(slots_of(kind)):
            index = index_of(d, slot)
            for cb in range(4 if slot < whole else 3):
                value = picked(d, cb, slot, *index)
                if slot >= whole:
                    value = jnp.where(lane < SHORT, value, spare[d, cb])
                if cb < 3:
                    out[d, slot * 24 + cb * 8 : slot * 24 + cb * 8 + 8, :] = value
                else:
                    row = 24 * slots_of(kind) + 3 * slot
                    out[d, row : row + 3, :] = value[0:3]


def compact(kind, mixed, low, high, depth, halo_coef, pick):
    return pl.pallas_call(
        functools.partial(compact_kernel, kind),
        out_shape=jax.ShapeDtypeStruct((OWNERS, block_rows(kind), LANES), jnp.float32),
        in_specs=[VMEM] * 6,
        out_specs=VMEM,
        scratch_shapes=[
            pltpu.VMEM((4, PAD, COLS), jnp.float32),
            pltpu.VMEM((OWNERS, 2, PAD, LANES), jnp.float32),
            pltpu.VMEM((OWNERS, 3, 8, LANES), jnp.float32),
            pltpu.VMEM((OWNERS, 8, LANES), jnp.float32),
        ],
        compiler_params=PARAMS,
        cost_estimate=pl.CostEstimate(flops=5000000, bytes_accessed=4000000, transcendentals=0),
        name="compact",
    )(mixed, low, high, depth, halo_coef, pick)


def runs():
    found = []
    for s in range(OWNERS):
        k = 0
        while k < HELD:
            c = s * HELD + k
            end = min(24 if k < 24 else HELD, k + NTH - c % NTH)
            found.append((s, k, end - k, c))
            k = end
    return found


def columns(vector):
    pieces = []
    for begin in range(0, vector.shape[0], LANES):
        size = min(LANES, vector.shape[0] - begin)
        row = jnp.broadcast_to(vector[begin : begin + size][None, :], (8, size))
        if size < LANES:
            row = jnp.concatenate([row, jnp.zeros((8, LANES - size), jnp.float32)], axis=1)
        column = jnp.transpose(row)[:size, 0:1]
        pieces.append(jnp.broadcast_to(column, (size, LANES)))
    return pieces


def source_kernel(
    kind, points, turn_own, refraction, growth, dissipation, first_far, second_far, out,
    grid, turned, low, pair,
):
    first, second = first_far, second_far
    whole = kind[0]
    tiles = slots_of(kind)
    ncomp = low.shape[0]
    nfreq = ncomp // NTH
    width = NTH + 4
    for slot in range(tiles):
        lanes = slice(slot * LANES, (slot + 1) * LANES)
        for s, k, size, c in runs():
            to = c // NTH * width + 2 + c % NTH
            if k >= 24 and slot >= whole:
                for i in range(k - 24, k - 24 + size):
                    row = slot * 24 + i * 8
                    grid[slot, to : to + 1, :] = untuck(points[s, row : row + 8, :])[0:1]
                    to += 1
                continue
            row = slot * 24 + k if k < 24 else 24 * tiles + 3 * slot + k - 24
            grid[slot, to : to + size, :] = points[s, row : row + size, :]
        for f in range(nfreq):
            base = f * width
            grid[slot, base : base + 2, :] = grid[slot, base + NTH : base + NTH + 2, :]
            grid[slot, base + NTH + 2 : base + NTH + 4, :] = grid[slot, base + 2 : base + 4, :]
        turn_row = jnp.broadcast_to(turn_own[0:1, lanes], (8, LANES))
        up = turn_row >= 0.0
        sixth = turn_row / 6.0
        by_turn = [
            sixth * jnp.where(up, 3.0, -3.0),
            sixth * jnp.where(up, 2.0, 6.0),
            sixth * jnp.where(up, -6.0, -2.0),
            jnp.where(up, sixth, -sixth),
        ]
        for f in range(nfreq):
            base = f * width
            c0, ca, cb, cf = [c * refraction[f] for c in by_turn]
            for begin in range(0, NTH, 8):
                size = min(8, NTH - begin)
                at = base + 2 + begin

                def near(step):
                    return grid[slot, at + step : at + step + size, :]

                centre = near(0)
                total = c0[:size] * centre + ca[:size] * near(1) + cb[:size] * near(-1)
                total += cf[:size] * jnp.where(up[:size], near(-2), near(2))
                to = f * NTH + begin
                turned[slot, to : to + size, :] = centre - total

    energy = []
    for slot in range(tiles):
        value = turned[slot]
        low[:, slot * LANES : (slot + 1) * LANES] = value.astype(jnp.bfloat16)
        energy.append(jnp.sum(value, axis=0, keepdims=True) / ncomp)
    keep = [1.0 + 0.2 * column for column in columns(growth)]
    lose = [0.2 * column for column in columns(dissipation)]
    partner = jnp.dot(first[...], low[...], preferred_element_type=jnp.float32)
    for slot in range(tiles):
        lanes = slice(slot * LANES, (slot + 1) * LANES)
        pair[:, lanes] = (turned[slot] * partner[:, lanes]).astype(jnp.bfloat16)
    nonlinear = jnp.dot(second[...], pair[...], preferred_element_type=jnp.float32)
    for slot in range(tiles):
        lanes = slice(slot * LANES, (slot + 1) * LANES)
        for begin in range(0, ncomp, LANES):
            part = slice(begin, min(begin + LANES, ncomp))
            scale = keep[begin // LANES] - lose[begin // LANES] * energy[slot]
            turned[slot, part, :] = turned[slot, part, :] * scale + 0.2 * nonlinear[part, lanes]
    lane = iota((8, LANES), 1)
    for s in range(OWNERS):
        for slot in range(tiles):
            c = s * HELD
            if slot < whole:
                out[s, slot * 24 : slot * 24 + 24, :] = turned[slot, c : c + 24, :]
                row = 24 * tiles + 3 * slot
                out[s, row : row + 3, :] = turned[slot, c + 24 : c + HELD, :]
                continue
            for cb in range(3):
                value = turned[slot, c + cb * 8 : c + cb * 8 + 8, :]
                spare = tuck(turned[slot, c + 24 + cb : c + 25 + cb, :])
                row = slot * 24 + cb * 8
                out[s, row : row + 8, :] = jnp.where(lane < SHORT, value, spare)


def sources(kind, points, turn_own, refraction, growth, dissipation, first, second):
    ncomp = first.shape[0]
    tiles = slots_of(kind)
    lanes = tiles * LANES
    return pl.pallas_call(
        functools.partial(source_kernel, kind),
        out_shape=jax.ShapeDtypeStruct(points.shape, jnp.float32),
        in_specs=[VMEM, VMEM, SMEM, VMEM, VMEM, VMEM, VMEM],
        out_specs=VMEM,
        scratch_shapes=[
            pltpu.VMEM((tiles, ncomp // NTH * (NTH + 4), LANES), jnp.float32),
            pltpu.VMEM((tiles, ncomp, LANES), jnp.float32),
            pltpu.VMEM((ncomp, lanes), jnp.bfloat16),
            pltpu.VMEM((ncomp, lanes), jnp.bfloat16),
        ],
        compiler_params=PARAMS,
        cost_estimate=pl.CostEstimate(
            flops=4 * ncomp * ncomp * lanes, bytes_accessed=6000000, transcendentals=0
        ),
        name="sources",
    )(points, turn_own, refraction, growth, dissipation, first, second)


def expand_kernel(kind, result, rank, mixed, last):
    whole, short = kind
    slots = slots_of(kind)
    tail_rows = (3 * whole + 7) // 8 * 8
    row_at = iota((8, LANES), 0)

    def short_step(d):
        row = whole * 24
        parts = [untuck(result[d, row + cb * 8 : row + cb * 8 + 8, :]) for cb in range(3)]
        value = jnp.where(row_at == 1, parts[1], parts[0])
        last[d] = jnp.where(row_at == 2, parts[2], value)

    def owner_step(d, rank_row):
        tail = result[d, 24 * slots : 24 * slots + tail_rows, :]
        values = []
        for slot in range(slots):
            parts = [result[d, slot * 24 + cb * 8 : slot * 24 + cb * 8 + 8, :] for cb in range(3)]
            if slot < whole:
                parts.append(pltpu.roll(tail, (tail_rows - 3 * slot) % tail_rows, axis=0)[0:8])
            else:
                parts.append(last[d])
            values.append(parts)
        for t in range(TILES):
            index = jnp.broadcast_to(rank_row[:, t * LANES : (t + 1) * LANES], (8, LANES))
            slot_of = index >> 7
            land = index < 0
            index = index & (LANES - 1)
            for cb in range(4):
                total = lane_gather(values[0][cb], index)
                for slot in range(1, min(t + 1, slots)):
                    total = jnp.where(slot_of == slot, lane_gather(values[slot][cb], index), total)
                mixed[d, cb * 8 : cb * 8 + 8, t * LANES : (t + 1) * LANES] = jnp.where(
                    land, 0.0, total
                )

    if short:
        for d in range(OWNERS):
            short_step(d)
    for d in range(OWNERS):
        owner_step(d, rank[d : d + 1, :])


def expand(kind, result, rank):
    return pl.pallas_call(
        functools.partial(expand_kernel, kind),
        out_shape=jax.ShapeDtypeStruct((OWNERS, PAD, COLS), jnp.float32),
        in_specs=[VMEM] * 2,
        out_specs=VMEM,
        scratch_shapes=[pltpu.VMEM((OWNERS, 8, LANES), jnp.float32)],
        compiler_params=PARAMS,
        cost_estimate=pl.CostEstimate(flops=5000000, bytes_accessed=4000000, transcendentals=0),
        name="expand",
    )(result, rank)


def finish_kernel(mixed, out, done, leaving):
    lane = iota((8, LANES), 1)
    copies = []
    for cb in range(4):
        size = min(8, HELD - cb * 8)
        for g in range(4):
            for t in range(TILES):
                lanes = slice(t * LANES, (t + 1) * LANES)
                rows = [mixed[(g ^ t) * 8 + j, cb * 8 : cb * 8 + 8, lanes] for j in range(8)]
                block = jnp.swapaxes(jnp.stack(butterfly(rows, lane)), 0, 1)
                done[cb * 8 : cb * 8 + size, g * 8 : g * 8 + 8, lanes] = block[0:size]
        part = slice(cb * 8, cb * 8 + size)
        copies.append(pltpu.make_async_copy(done.at[part], out.at[part], leaving.at[cb]))
        copies[cb].start()
    for copy in copies:
        copy.wait()


def finish(mixed):
    return pl.pallas_call(
        finish_kernel,
        out_shape=jax.ShapeDtypeStruct((HELD, ROWS, COLS), jnp.float32),
        in_specs=[VMEM],
        out_specs=ANY,
        scratch_shapes=[
            pltpu.VMEM((HELD, ROWS, COLS), jnp.float32),
            pltpu.SemaphoreType.DMA((4,)),
        ],
        compiler_params=PARAMS,
        cost_estimate=pl.CostEstimate(flops=5000000, bytes_accessed=4000000, transcendentals=0),
        name="finish",
    )(mixed)


def exchange(blocks):
    return lax.all_to_all(blocks, "comp", split_axis=0, concat_axis=0, tiled=True)


def shards(
    spectrum, speed, depth, turn, sea_mask, refraction, growth, dissipation, quad_first, quad_second
):
    count = lax.axis_size("tile")
    forward = [(i, i + 1) for i in range(count - 1)]
    backward = [(i + 1, i) for i in range(count - 1)]
    grid, first, last = prepare(spectrum)
    low = lax.ppermute(last, "tile", forward)
    high = lax.ppermute(first, "tile", backward)
    mixed, halo_coef, pick, rank, turn_own, chosen = propagate(
        grid, depth, turn, sea_mask, speed
    )

    def rest(kind):
        def run(mixed, low, high):
            sent = compact(kind, mixed, low, high, depth, halo_coef, pick)
            points = exchange(sent)
            result = sources(
                kind, points, turn_own, refraction, growth, dissipation, quad_first, quad_second
            )
            return expand(kind, exchange(result), rank)

        return run

    return finish(lax.switch(chosen[0], [rest(kind) for kind in KINDS], mixed, low, high))


def solution(mesh):
    in_specs = (
        P("comp", "tile", None),
        P("comp"),
        P("tile", None),
        P("tile", None),
        P("tile", None),
        P(),
        P(),
        P(),
        P(),
        P(),
    )
    out_specs = P("comp", "tile", None)
    return jax.shard_map(shards, mesh=mesh, in_specs=in_specs, out_specs=out_specs, check_vma=False)
```

```python
import functools
import math

import jax
import jax.numpy as jnp
from jax import lax
from jax.experimental import pallas as pl
from jax.experimental.pallas import tpu as pltpu
from jax.sharding import PartitionSpec as P

NTH = 36
HELD = 27
PAD = 32
ROWS = 32
COLS = 512
OWNERS = 32
LANES = 128
TILES = COLS // LANES
VMEM = pl.BlockSpec(memory_space=pltpu.VMEM)
SMEM = pl.BlockSpec(memory_space=pltpu.SMEM)
ANY = pl.BlockSpec(memory_space=pl.ANY)
PARAMS = pltpu.CompilerParams(vmem_limit_bytes=24 * 2**20)


def iota(shape, dim):
    return lax.broadcasted_iota(jnp.int32, shape, dim)


def lane_gather(values, index):
    return jnp.take_along_axis(values, index, axis=1, mode="promise_in_bounds")


def wide(coef):
    return jnp.concatenate([coef] * TILES, axis=1)


def butterfly(rows, lane):
    for step, bit in ((1, 16), (2, 32), (4, 64)):
        swap = (lane & bit) != 0
        rows = [jnp.where(swap, rows[j ^ step], rows[j]) for j in range(8)]
    return rows


def mixed_plane(plane):
    lane = iota((ROWS, LANES), 1)
    row = iota((ROWS, LANES), 0)
    pieces = []
    for t in range(TILES):
        block = plane[:, t * LANES : (t + 1) * LANES]
        block = jnp.concatenate([block[(g ^ t) * 8 : (g ^ t) * 8 + 8] for g in range(4)], axis=0)
        for step, bit in ((1, 16), (2, 32), (4, 64)):
            swapped = jnp.where(
                (row & step) != 0,
                pltpu.roll(block, step, axis=0),
                pltpu.roll(block, ROWS - step, axis=0),
            )
            block = jnp.where((lane & bit) != 0, swapped, block)
        pieces.append(block)
    return jnp.concatenate(pieces, axis=1)


def prepare_kernel(spec, grid, to_pair, to_other):
    for cb in range(4):
        part = slice(cb * 8, cb * 8 + 8)
        size = min(8, HELD - cb * 8)
        for rb in range(4):
            block = spec[cb * 8 : cb * 8 + size, rb * 8 : rb * 8 + 8, :]
            if size < 8:
                block = jnp.concatenate(
                    [block, jnp.zeros((8 - size, 8, COLS), jnp.float32)], axis=0
                )
            grid[rb * 8 : rb * 8 + 8, part, :] = jnp.swapaxes(block, 0, 1)
    odd = lax.rem(lax.axis_index("tile"), 2)
    to_pair[...] = grid[pl.ds((1 - odd) * (ROWS - 2), 2), :, :]
    to_other[...] = grid[pl.ds(odd * (ROWS - 2), 2), :, :]


def prepare(spectrum):
    edge = jax.ShapeDtypeStruct((2, PAD, COLS), jnp.float32)
    return pl.pallas_call(
        prepare_kernel,
        out_shape=[jax.ShapeDtypeStruct((ROWS, PAD, COLS), jnp.float32), edge, edge],
        in_specs=[VMEM],
        out_specs=[VMEM] * 3,
        compiler_params=PARAMS,
        cost_estimate=pl.CostEstimate(flops=2000000, bytes_accessed=4000000, transcendentals=0),
        name="prepare",
    )(spectrum)


def index_steps(me, turn, mask, pick, rank, turn_own, chosen):
    sea = mixed_plane(mask[...])
    yield
    column = iota((ROWS, COLS), 1)
    count = sea
    step = 1
    while step < COLS:
        count = count + jnp.where(column >= step, pltpu.roll(count, step, axis=1), 0)
        step *= 2
        if step <= LANES:
            yield
    largest = jnp.max(count)
    kind = jnp.int32(0)
    for whole, short in KINDS[:-1]:
        kind += (largest > whole * LANES + short).astype(jnp.int32)
    chosen[0] = kind
    place = count - 1
    rank[...] = jnp.where(sea > 0, place, -1)
    entry = jnp.where(sea > 0, column * COLS + (column - place), -1)
    step = 1
    while step < COLS:
        other = pltpu.roll(entry, COLS - step, axis=1)
        arrives = (other >= 0) & ((other & step) != 0)
        stays = (entry >= 0) & ((entry & step) == 0)
        entry = jnp.where(arrives, other, jnp.where(stays, entry, -1))
        step *= 2
        if step <= LANES:
            yield
    entry = jnp.where(entry >= 0, entry >> 9, 0)
    pick[...] = entry
    mine = iota((ROWS, COLS), 0) == me
    own_turn = jnp.sum(jnp.where(mine, mixed_plane(turn[...]), 0.0), axis=0, keepdims=True)
    own_pick = jnp.sum(jnp.where(mine, entry, 0), axis=0, keepdims=True)
    for t in range(TILES):
        index = jnp.broadcast_to(own_pick[:, t * LANES : (t + 1) * LANES], (8, LANES))
        total = jnp.zeros((8, LANES), jnp.float32)
        for source in range(TILES):
            own = jnp.broadcast_to(own_turn[:, source * LANES : (source + 1) * LANES], (8, LANES))
            value = lane_gather(own, index & (LANES - 1))
            total = jnp.where(index >> 7 == source, value, total)
        turn_own[:, t * LANES : (t + 1) * LANES] = total
    yield


def shifted(tiles, lane, far_lane, take_back, take_ahead):
    ahead = [pltpu.roll(v, LANES - 1, axis=1) for v in tiles] + [0.0]
    back = [0.0] + [pltpu.roll(v, 1, axis=1) for v in tiles]
    far = [0.0] + [lane_gather(v, far_lane) for v in tiles] + [0.0]
    return [
        (
            jnp.where(lane < LANES - 1, ahead[t], ahead[t + 1]),
            jnp.where(lane >= 1, back[t + 1], back[t]),
            jnp.where(take_back, far[t], jnp.where(take_ahead, far[t + 2], far[t + 1])),
        )
        for t in range(TILES)
    ]


def propagate_kernel(
    grid, depth, turn, mask, speed, mixed, halo_coef, pick, rank, turn_own, chosen
):
    me = lax.axis_index("comp")
    beside = index_steps(me, turn, mask, pick, rank, turn_own, chosen)
    sub = iota((PAD, LANES), 0)
    speeds = jnp.zeros((PAD, LANES), jnp.float32)
    for k in range(HELD):
        speeds = jnp.where(sub == k, speed[k], speeds)
    theta = (2.0 * math.pi / NTH) * lax.rem(me * HELD + sub, NTH).astype(jnp.float32)

    def taps(velocity):
        up = velocity >= 0.0
        sixth = velocity / 6.0
        return (
            sixth * jnp.where(up, 3.0, -3.0),
            sixth * jnp.where(up, 2.0, 6.0),
            sixth * jnp.where(up, -6.0, -2.0),
            jnp.where(up, sixth, -sixth),
            up,
        )

    x_centre, x_ahead, x_back, x_far, x_up = taps(speeds * jnp.cos(theta))
    y_centre, y_ahead, y_back, y_far, y_up = taps(speeds * jnp.sin(theta))
    halo_coef[0] = y_back
    halo_coef[1] = jnp.where(y_up, y_far, 0.0)
    halo_coef[2] = y_ahead
    halo_coef[3] = jnp.where(y_up, 0.0, y_far)
    centre_coef = x_centre + y_centre

    lane = iota((8, LANES), 1)
    for cb in range(4):
        part = slice(cb * 8, cb * 8 + 8)
        c0, xa, xb, xf, xu, ya, yb, yf, yu = [
            c[part]
            for c in (centre_coef, x_ahead, x_back, x_far, x_up, y_ahead, y_back, y_far, y_up)
        ]

        far_from = (
            (lane + jnp.where(xu, LANES - 2, 2)) & (LANES - 1),
            xu & (lane < 2),
            jnp.logical_not(xu) & (lane >= LANES - 2),
        )

        def row_step(r, rows, depth_row):
            results = []
            centre = [grid[r, part, t * LANES : (t + 1) * LANES] for t in range(TILES)]

            def near(i, t):
                if not 0 <= rows + i < ROWS:
                    return jnp.zeros((8, LANES), jnp.float32)
                return grid[r + i, part, t * LANES : (t + 1) * LANES]

            for t, (ahead, back, far) in enumerate(shifted(centre, lane, *far_from)):
                total = c0 * centre[t] + xa * ahead + xb * back
                total += xf * far
                total += ya * near(1, t) + yb * near(-1, t)
                total += yf * jnp.where(yu, near(-2, t), near(2, t))
                lanes = slice(t * LANES, (t + 1) * LANES)
                results.append(centre[t] - depth_row[:, lanes] * total)
            return results

        for rb in range(ROWS // 8):
            depths = depth[rb * 8 : rb * 8 + 8, :]
            group = [row_step(rb * 8 + i, rb * 8 + i, depths[i : i + 1, :]) for i in range(8)]
            for t in range(TILES):
                for j, value in enumerate(butterfly([row[t] for row in group], lane)):
                    mixed[(rb ^ t) * 8 + j, part, t * LANES : (t + 1) * LANES] = value
            next(beside, None)
    for _ in beside:
        pass


def propagate(grid, depth, turn, mask, speed):
    plane = jax.ShapeDtypeStruct((ROWS, COLS), jnp.int32)
    return pl.pallas_call(
        propagate_kernel,
        out_shape=[
            jax.ShapeDtypeStruct((ROWS, PAD, COLS), jnp.float32),
            jax.ShapeDtypeStruct((4, PAD, LANES), jnp.float32),
            plane,
            plane,
            jax.ShapeDtypeStruct((8, COLS), jnp.float32),
            jax.ShapeDtypeStruct((1,), jnp.int32),
        ],
        in_specs=[VMEM, VMEM, VMEM, VMEM, SMEM],
        out_specs=[VMEM] * 5 + [SMEM],
        compiler_params=PARAMS,
        cost_estimate=pl.CostEstimate(flops=20000000, bytes_accessed=4000000, transcendentals=0),
        name="propagate",
    )(grid, depth, turn, mask, speed)


SHORT = 112
KINDS = ((2, SHORT), (3, 0), (4, 0))


def slots_of(kind):
    return kind[0] + (kind[1] > 0)


def block_rows(kind):
    return (24 * slots_of(kind) + 3 * kind[0] + 7) // 8 * 8


def tuck(row):
    spare = iota((8, LANES), 0) * 16 + (iota((8, LANES), 1) & 15)
    return lane_gather(jnp.broadcast_to(row, (8, LANES)), spare)


def untuck(rows):
    lane = iota((8, LANES), 1)
    value = lane_gather(rows, SHORT + (lane & 15))
    value = jnp.where(iota((8, LANES), 0) == lane >> 4, value, 0.0)
    for step in (4, 2, 1):
        value = value + pltpu.roll(value, step, axis=0)
    return value


def compact_kernel(kind, mixed, from_pair, from_other, depth, halo_coef, pick, out, terms, fixed, spare, tails):
    lane = iota((8, LANES), 1)
    strip = lane >> 4
    back, back_two, ahead, ahead_two = [wide(halo_coef[i]) for i in range(4)]
    odd = lax.rem(lax.axis_index("tile"), 2) == 1
    low = [jnp.where(odd, from_pair[i], from_other[i]) for i in range(2)]
    high = [jnp.where(odd, from_other[i], from_pair[i]) for i in range(2)]
    terms[0] = depth[0:1, :] * (back * low[1] + back_two * low[0])
    terms[1] = depth[1:2, :] * (back_two * low[1])
    terms[2] = depth[ROWS - 2 : ROWS - 1, :] * (ahead_two * high[0])
    terms[3] = depth[ROWS - 1 : ROWS, :] * (ahead * high[0] + ahead_two * high[1])

    for g in range(4):
        for first, row, t in ((0, 0, g), (2, 6, 3 - g)):
            lanes = slice(t * LANES, (t + 1) * LANES)
            for cb in range(4):
                part = slice(cb * 8, cb * 8 + 8)
                one, two = terms[first, part, lanes], terms[first + 1, part, lanes]
                for j in range(8):
                    term = jnp.where(strip == (row + 1) ^ j, two, 0.0)
                    term = jnp.where(strip == row ^ j, one, term)
                    fixed[g * 8 + j, first // 2, part, :] = mixed[g * 8 + j, part, lanes] - term

    whole, short = kind

    def load(d, cb, t):
        part = slice(cb * 8, cb * 8 + 8)
        if t == d // 8:
            return fixed[d, 0, part, :]
        if t == 3 - d // 8:
            return fixed[d, 1, part, :]
        return mixed[d, part, t * LANES : (t + 1) * LANES]

    def index_of(d, slot):
        index = jnp.broadcast_to(pick[d : d + 1, slot * LANES : (slot + 1) * LANES], (8, LANES))
        return index & (LANES - 1), [index >> 7 == t for t in range(TILES)]

    def picked(d, cb, slot, index, among):
        total = lane_gather(load(d, cb, slot), index)
        for source in range(slot + 1, TILES):
            value = lane_gather(load(d, cb, source), index)
            total = jnp.where(among[source], value, total)
        return total

    if short:
        for d in range(OWNERS):
            tails[d] = picked(d, 3, whole, *index_of(d, whole))
        for d in range(OWNERS):
            for cb in range(3):
                spare[d, cb] = tuck(tails[d, cb : cb + 1, :])

    for d in range(OWNERS):
        for slot in range(slots_of(kind)):
            index = index_of(d, slot)
            for cb in range(4 if slot < whole else 3):
                value = picked(d, cb, slot, *index)
                if slot >= whole:
                    value = jnp.where(lane < SHORT, value, spare[d, cb])
                if cb < 3:
                    out[d, slot * 24 + cb * 8 : slot * 24 + cb * 8 + 8, :] = value
                else:
                    row = 24 * slots_of(kind) + 3 * slot
                    out[d, row : row + 3, :] = value[0:3]


def compact(kind, mixed, from_pair, from_other, depth, halo_coef, pick):
    return pl.pallas_call(
        functools.partial(compact_kernel, kind),
        out_shape=jax.ShapeDtypeStruct((OWNERS, block_rows(kind), LANES), jnp.float32),
        in_specs=[VMEM] * 6,
        out_specs=VMEM,
        scratch_shapes=[
            pltpu.VMEM((4, PAD, COLS), jnp.float32),
            pltpu.VMEM((OWNERS, 2, PAD, LANES), jnp.float32),
            pltpu.VMEM((OWNERS, 3, 8, LANES), jnp.float32),
            pltpu.VMEM((OWNERS, 8, LANES), jnp.float32),
        ],
        compiler_params=PARAMS,
        cost_estimate=pl.CostEstimate(flops=5000000, bytes_accessed=4000000, transcendentals=0),
        name="compact",
    )(mixed, from_pair, from_other, depth, halo_coef, pick)


def runs():
    found = []
    for s in range(OWNERS):
        k = 0
        while k < HELD:
            c = s * HELD + k
            end = min(24 if k < 24 else HELD, k + NTH - c % NTH)
            found.append((s, k, end - k, c))
            k = end
    return found


def columns(vector):
    pieces = []
    for begin in range(0, vector.shape[0], LANES):
        size = min(LANES, vector.shape[0] - begin)
        row = jnp.broadcast_to(vector[begin : begin + size][None, :], (8, size))
        if size < LANES:
            row = jnp.concatenate([row, jnp.zeros((8, LANES - size), jnp.float32)], axis=1)
        column = jnp.transpose(row)[:size, 0:1]
        pieces.append(jnp.broadcast_to(column, (size, LANES)))
    return pieces


def source_kernel(
    kind, points, turn_own, refraction, growth, dissipation, first_far, second_far, out,
    grid, turned, low, pair,
):
    first, second = first_far, second_far
    whole = kind[0]
    tiles = slots_of(kind)
    ncomp = low.shape[0]
    nfreq = ncomp // NTH
    width = NTH + 4
    for slot in range(tiles):
        lanes = slice(slot * LANES, (slot + 1) * LANES)
        for s, k, size, c in runs():
            to = c // NTH * width + 2 + c % NTH
            if k >= 24 and slot >= whole:
                for i in range(k - 24, k - 24 + size):
                    row = slot * 24 + i * 8
                    grid[slot, to : to + 1, :] = untuck(points[s, row : row + 8, :])[0:1]
                    to += 1
                continue
            row = slot * 24 + k if k < 24 else 24 * tiles + 3 * slot + k - 24
            grid[slot, to : to + size, :] = points[s, row : row + size, :]
        for f in range(nfreq):
            base = f * width
            grid[slot, base : base + 2, :] = grid[slot, base + NTH : base + NTH + 2, :]
            grid[slot, base + NTH + 2 : base + NTH + 4, :] = grid[slot, base + 2 : base + 4, :]
        turn_row = jnp.broadcast_to(turn_own[0:1, lanes], (8, LANES))
        up = turn_row >= 0.0
        sixth = turn_row / 6.0
        by_turn = [
            sixth * jnp.where(up, 3.0, -3.0),
            sixth * jnp.where(up, 2.0, 6.0),
            sixth * jnp.where(up, -6.0, -2.0),
            jnp.where(up, sixth, -sixth),
        ]
        for f in range(nfreq):
            base = f * width
            c0, ca, cb, cf = [c * refraction[f] for c in by_turn]
            for begin in range(0, NTH, 8):
                size = min(8, NTH - begin)
                at = base + 2 + begin

                def near(step):
                    return grid[slot, at + step : at + step + size, :]

                centre = near(0)
                total = c0[:size] * centre + ca[:size] * near(1) + cb[:size] * near(-1)
                total += cf[:size] * jnp.where(up[:size], near(-2), near(2))
                to = f * NTH + begin
                turned[slot, to : to + size, :] = centre - total

    energy = []
    for slot in range(tiles):
        value = turned[slot]
        low[:, slot * LANES : (slot + 1) * LANES] = value.astype(jnp.bfloat16)
        energy.append(jnp.sum(value, axis=0, keepdims=True) / ncomp)
    keep = [1.0 + 0.2 * column for column in columns(growth)]
    lose = [0.2 * column for column in columns(dissipation)]
    partner = jnp.dot(first[...], low[...], preferred_element_type=jnp.float32)
    for slot in range(tiles):
        lanes = slice(slot * LANES, (slot + 1) * LANES)
        pair[:, lanes] = (turned[slot] * partner[:, lanes]).astype(jnp.bfloat16)
    nonlinear = jnp.dot(second[...], pair[...], preferred_element_type=jnp.float32)
    for slot in range(tiles):
        lanes = slice(slot * LANES, (slot + 1) * LANES)
        for begin in range(0, ncomp, LANES):
            part = slice(begin, min(begin + LANES, ncomp))
            scale = keep[begin // LANES] - lose[begin // LANES] * energy[slot]
            turned[slot, part, :] = turned[slot, part, :] * scale + 0.2 * nonlinear[part, lanes]
    lane = iota((8, LANES), 1)
    for s in range(OWNERS):
        for slot in range(tiles):
            c = s * HELD
            if slot < whole:
                out[s, slot * 24 : slot * 24 + 24, :] = turned[slot, c : c + 24, :]
                row = 24 * tiles + 3 * slot
                out[s, row : row + 3, :] = turned[slot, c + 24 : c + HELD, :]
                continue
            for cb in range(3):
                value = turned[slot, c + cb * 8 : c + cb * 8 + 8, :]
                spare = tuck(turned[slot, c + 24 + cb : c + 25 + cb, :])
                row = slot * 24 + cb * 8
                out[s, row : row + 8, :] = jnp.where(lane < SHORT, value, spare)


def sources(kind, points, turn_own, refraction, growth, dissipation, first, second):
    ncomp = first.shape[0]
    tiles = slots_of(kind)
    lanes = tiles * LANES
    return pl.pallas_call(
        functools.partial(source_kernel, kind),
        out_shape=jax.ShapeDtypeStruct(points.shape, jnp.float32),
        in_specs=[VMEM, VMEM, SMEM, VMEM, VMEM, VMEM, VMEM],
        out_specs=VMEM,
        scratch_shapes=[
            pltpu.VMEM((tiles, ncomp // NTH * (NTH + 4), LANES), jnp.float32),
            pltpu.VMEM((tiles, ncomp, LANES), jnp.float32),
            pltpu.VMEM((ncomp, lanes), jnp.bfloat16),
            pltpu.VMEM((ncomp, lanes), jnp.bfloat16),
        ],
        compiler_params=PARAMS,
        cost_estimate=pl.CostEstimate(
            flops=4 * ncomp * ncomp * lanes, bytes_accessed=6000000, transcendentals=0
        ),
        name="sources",
    )(points, turn_own, refraction, growth, dissipation, first, second)


def expand_kernel(kind, result, rank, mixed, last):
    whole, short = kind
    slots = slots_of(kind)
    tail_rows = (3 * whole + 7) // 8 * 8
    row_at = iota((8, LANES), 0)

    def short_step(d):
        row = whole * 24
        parts = [untuck(result[d, row + cb * 8 : row + cb * 8 + 8, :]) for cb in range(3)]
        value = jnp.where(row_at == 1, parts[1], parts[0])
        last[d] = jnp.where(row_at == 2, parts[2], value)

    def owner_step(d, rank_row):
        tail = result[d, 24 * slots : 24 * slots + tail_rows, :]
        values = []
        for slot in range(slots):
            parts = [result[d, slot * 24 + cb * 8 : slot * 24 + cb * 8 + 8, :] for cb in range(3)]
            if slot < whole:
                parts.append(pltpu.roll(tail, (tail_rows - 3 * slot) % tail_rows, axis=0)[0:8])
            else:
                parts.append(last[d])
            values.append(parts)
        for t in range(TILES):
            index = jnp.broadcast_to(rank_row[:, t * LANES : (t + 1) * LANES], (8, LANES))
            slot_of = index >> 7
            land = index < 0
            index = index & (LANES - 1)
            for cb in range(4):
                total = lane_gather(values[0][cb], index)
                for slot in range(1, min(t + 1, slots)):
                    total = jnp.where(slot_of == slot, lane_gather(values[slot][cb], index), total)
                mixed[d, cb * 8 : cb * 8 + 8, t * LANES : (t + 1) * LANES] = jnp.where(
                    land, 0.0, total
                )

    if short:
        for d in range(OWNERS):
            short_step(d)
    for d in range(OWNERS):
        owner_step(d, rank[d : d + 1, :])


def expand(kind, result, rank):
    return pl.pallas_call(
        functools.partial(expand_kernel, kind),
        out_shape=jax.ShapeDtypeStruct((OWNERS, PAD, COLS), jnp.float32),
        in_specs=[VMEM] * 2,
        out_specs=VMEM,
        scratch_shapes=[pltpu.VMEM((OWNERS, 8, LANES), jnp.float32)],
        compiler_params=PARAMS,
        cost_estimate=pl.CostEstimate(flops=5000000, bytes_accessed=4000000, transcendentals=0),
        name="expand",
    )(result, rank)


def finish_kernel(mixed, out, done, leaving):
    lane = iota((8, LANES), 1)
    copies = []
    for cb in range(4):
        size = min(8, HELD - cb * 8)
        for g in range(4):
            for t in range(TILES):
                lanes = slice(t * LANES, (t + 1) * LANES)
                rows = [mixed[(g ^ t) * 8 + j, cb * 8 : cb * 8 + 8, lanes] for j in range(8)]
                block = jnp.swapaxes(jnp.stack(butterfly(rows, lane)), 0, 1)
                done[cb * 8 : cb * 8 + size, g * 8 : g * 8 + 8, lanes] = block[0:size]
        part = slice(cb * 8, cb * 8 + size)
        copies.append(pltpu.make_async_copy(done.at[part], out.at[part], leaving.at[cb]))
        copies[cb].start()
    for copy in copies:
        copy.wait()


def finish(mixed):
    return pl.pallas_call(
        finish_kernel,
        out_shape=jax.ShapeDtypeStruct((HELD, ROWS, COLS), jnp.float32),
        in_specs=[VMEM],
        out_specs=ANY,
        scratch_shapes=[
            pltpu.VMEM((HELD, ROWS, COLS), jnp.float32),
            pltpu.SemaphoreType.DMA((4,)),
        ],
        compiler_params=PARAMS,
        cost_estimate=pl.CostEstimate(flops=5000000, bytes_accessed=4000000, transcendentals=0),
        name="finish",
    )(mixed)


def exchange(blocks):
    return lax.all_to_all(blocks, "comp", split_axis=0, concat_axis=0, tiled=True)


def shards(
    spectrum, speed, depth, turn, sea_mask, refraction, growth, dissipation, quad_first, quad_second
):
    count = lax.axis_size("tile")

    def swap(rows, begin):
        pairs = [(i, i + 1) for i in range(begin, count - 1, 2)]
        return lax.ppermute(rows, "tile", pairs + [(j, i) for i, j in pairs])

    grid, to_pair, to_other = prepare(spectrum)
    from_pair = swap(to_pair, 0)
    from_other = swap(to_other, 1)
    mixed, halo_coef, pick, rank, turn_own, chosen = propagate(
        grid, depth, turn, sea_mask, speed
    )

    def rest(kind):
        def run(mixed, from_pair, from_other):
            sent = compact(kind, mixed, from_pair, from_other, depth, halo_coef, pick)
            points = exchange(sent)
            result = sources(
                kind, points, turn_own, refraction, growth, dissipation, quad_first, quad_second
            )
            return expand(kind, exchange(result), rank)

        return run

    return finish(lax.switch(chosen[0], [rest(kind) for kind in KINDS], mixed, from_pair, from_other))


def solution(mesh):
    in_specs = (
        P("comp", "tile", None),
        P("comp"),
        P("tile", None),
        P("tile", None),
        P("tile", None),
        P(),
        P(),
        P(),
        P(),
        P(),
    )
    out_specs = P("comp", "tile", None)
    return jax.shard_map(shards, mesh=mesh, in_specs=in_specs, out_specs=out_specs, check_vma=False)
```

```python
import functools
import math

import jax
import jax.numpy as jnp
from jax import lax
from jax.experimental import pallas as pl
from jax.experimental.pallas import tpu as pltpu
from jax.sharding import PartitionSpec as P

NTH = 36
HELD = 27
PAD = 32
ROWS = 32
COLS = 512
OWNERS = 32
LANES = 128
TILES = COLS // LANES
VMEM = pl.BlockSpec(memory_space=pltpu.VMEM)
SMEM = pl.BlockSpec(memory_space=pltpu.SMEM)
ANY = pl.BlockSpec(memory_space=pl.ANY)
PARAMS = pltpu.CompilerParams(vmem_limit_bytes=24 * 2**20)


def iota(shape, dim):
    return lax.broadcasted_iota(jnp.int32, shape, dim)


def lane_gather(values, index):
    return jnp.take_along_axis(values, index, axis=1, mode="promise_in_bounds")


def wide(coef):
    return jnp.concatenate([coef] * TILES, axis=1)


def butterfly(rows, lane):
    for step, bit in ((1, 16), (2, 32), (4, 64)):
        swap = (lane & bit) != 0
        rows = [jnp.where(swap, rows[j ^ step], rows[j]) for j in range(8)]
    return rows


def mixed_plane(plane):
    lane = iota((ROWS, LANES), 1)
    row = iota((ROWS, LANES), 0)
    pieces = []
    for t in range(TILES):
        block = plane[:, t * LANES : (t + 1) * LANES]
        block = jnp.concatenate([block[(g ^ t) * 8 : (g ^ t) * 8 + 8] for g in range(4)], axis=0)
        for step, bit in ((1, 16), (2, 32), (4, 64)):
            swapped = jnp.where(
                (row & step) != 0,
                pltpu.roll(block, step, axis=0),
                pltpu.roll(block, ROWS - step, axis=0),
            )
            block = jnp.where((lane & bit) != 0, swapped, block)
        pieces.append(block)
    return jnp.concatenate(pieces, axis=1)


def prepare_kernel(spec, grid, to_pair, to_other):
    for cb in range(4):
        part = slice(cb * 8, cb * 8 + 8)
        size = min(8, HELD - cb * 8)
        for rb in range(4):
            block = spec[cb * 8 : cb * 8 + size, rb * 8 : rb * 8 + 8, :]
            if size < 8:
                block = jnp.concatenate(
                    [block, jnp.zeros((8 - size, 8, COLS), jnp.float32)], axis=0
                )
            grid[rb * 8 : rb * 8 + 8, part, :] = jnp.swapaxes(block, 0, 1)
    odd = lax.rem(lax.axis_index("tile"), 2)
    to_pair[...] = grid[pl.ds((1 - odd) * (ROWS - 2), 2), :, :]
    to_other[...] = grid[pl.ds(odd * (ROWS - 2), 2), :, :]


def prepare(spectrum):
    edge = jax.ShapeDtypeStruct((2, PAD, COLS), jnp.float32)
    return pl.pallas_call(
        prepare_kernel,
        out_shape=[jax.ShapeDtypeStruct((ROWS, PAD, COLS), jnp.float32), edge, edge],
        in_specs=[VMEM],
        out_specs=[VMEM] * 3,
        compiler_params=PARAMS,
        cost_estimate=pl.CostEstimate(flops=2000000, bytes_accessed=4000000, transcendentals=0),
        name="prepare",
    )(spectrum)


def index_steps(me, turn, mask, pick, rank, turn_own, chosen):
    sea = mixed_plane(mask[...])
    yield
    column = iota((ROWS, COLS), 1)
    count = sea
    step = 1
    while step < COLS:
        count = count + jnp.where(column >= step, pltpu.roll(count, step, axis=1), 0)
        step *= 2
        if step <= LANES:
            yield
    largest = jnp.max(count)
    kind = jnp.int32(0)
    for whole, short in KINDS[:-1]:
        kind += (largest > whole * LANES + short).astype(jnp.int32)
    chosen[0] = kind
    place = count - 1
    rank[...] = jnp.where(sea > 0, place, -1)
    entry = jnp.where(sea > 0, column * COLS + (column - place), -1)
    step = 1
    while step < COLS:
        other = pltpu.roll(entry, COLS - step, axis=1)
        arrives = (other >= 0) & ((other & step) != 0)
        stays = (entry >= 0) & ((entry & step) == 0)
        entry = jnp.where(arrives, other, jnp.where(stays, entry, -1))
        step *= 2
        if step <= LANES:
            yield
    entry = jnp.where(entry >= 0, entry >> 9, 0)
    pick[...] = entry
    mine = iota((ROWS, COLS), 0) == me
    own_turn = jnp.sum(jnp.where(mine, mixed_plane(turn[...]), 0.0), axis=0, keepdims=True)
    own_pick = jnp.sum(jnp.where(mine, entry, 0), axis=0, keepdims=True)
    for t in range(TILES):
        index = jnp.broadcast_to(own_pick[:, t * LANES : (t + 1) * LANES], (8, LANES))
        total = jnp.zeros((8, LANES), jnp.float32)
        for source in range(TILES):
            own = jnp.broadcast_to(own_turn[:, source * LANES : (source + 1) * LANES], (8, LANES))
            value = lane_gather(own, index & (LANES - 1))
            total = jnp.where(index >> 7 == source, value, total)
        turn_own[:, t * LANES : (t + 1) * LANES] = total
    yield


def shifted(tiles, lane, far_lane, take_back, take_ahead):
    ahead = [pltpu.roll(v, LANES - 1, axis=1) for v in tiles] + [0.0]
    back = [0.0] + [pltpu.roll(v, 1, axis=1) for v in tiles]
    far = [0.0] + [lane_gather(v, far_lane) for v in tiles] + [0.0]
    return [
        (
            jnp.where(lane < LANES - 1, ahead[t], ahead[t + 1]),
            jnp.where(lane >= 1, back[t + 1], back[t]),
            jnp.where(take_back, far[t], jnp.where(take_ahead, far[t + 2], far[t + 1])),
        )
        for t in range(TILES)
    ]


def propagate_kernel(
    grid, depth, turn, mask, speed, mixed, halo_coef, edge_depth, pick, rank, turn_own, chosen
):
    me = lax.axis_index("comp")
    beside = index_steps(me, turn, mask, pick, rank, turn_own, chosen)
    sub = iota((PAD, LANES), 0)
    speeds = jnp.zeros((PAD, LANES), jnp.float32)
    for k in range(HELD):
        speeds = jnp.where(sub == k, speed[k], speeds)
    theta = (2.0 * math.pi / NTH) * lax.rem(me * HELD + sub, NTH).astype(jnp.float32)

    def taps(velocity):
        up = velocity >= 0.0
        sixth = velocity / 6.0
        return (
            sixth * jnp.where(up, 3.0, -3.0),
            sixth * jnp.where(up, 2.0, 6.0),
            sixth * jnp.where(up, -6.0, -2.0),
            jnp.where(up, sixth, -sixth),
            up,
        )

    x_centre, x_ahead, x_back, x_far, x_up = taps(speeds * jnp.cos(theta))
    y_centre, y_ahead, y_back, y_far, y_up = taps(speeds * jnp.sin(theta))
    edge_depth[0:2, :] = depth[0:2, :]
    edge_depth[2:4, :] = depth[ROWS - 2 : ROWS, :]
    halo_coef[0] = y_back
    halo_coef[1] = jnp.where(y_up, y_far, 0.0)
    halo_coef[2] = y_ahead
    halo_coef[3] = jnp.where(y_up, 0.0, y_far)
    centre_coef = x_centre + y_centre

    lane = iota((8, LANES), 1)
    for cb in range(4):
        part = slice(cb * 8, cb * 8 + 8)
        c0, xa, xb, xf, xu, ya, yb, yf, yu = [
            c[part]
            for c in (centre_coef, x_ahead, x_back, x_far, x_up, y_ahead, y_back, y_far, y_up)
        ]

        far_from = (
            (lane + jnp.where(xu, LANES - 2, 2)) & (LANES - 1),
            xu & (lane < 2),
            jnp.logical_not(xu) & (lane >= LANES - 2),
        )

        def row_step(r, rows, depth_row):
            results = []
            centre = [grid[r, part, t * LANES : (t + 1) * LANES] for t in range(TILES)]

            def near(i, t):
                if not 0 <= rows + i < ROWS:
                    return jnp.zeros((8, LANES), jnp.float32)
                return grid[r + i, part, t * LANES : (t + 1) * LANES]

            for t, (ahead, back, far) in enumerate(shifted(centre, lane, *far_from)):
                total = c0 * centre[t] + xa * ahead + xb * back
                total += xf * far
                total += ya * near(1, t) + yb * near(-1, t)
                total += yf * jnp.where(yu, near(-2, t), near(2, t))
                lanes = slice(t * LANES, (t + 1) * LANES)
                results.append(centre[t] - depth_row[:, lanes] * total)
            return results

        for rb in range(ROWS // 8):
            depths = depth[rb * 8 : rb * 8 + 8, :]
            group = [row_step(rb * 8 + i, rb * 8 + i, depths[i : i + 1, :]) for i in range(8)]
            for t in range(TILES):
                for j, value in enumerate(butterfly([row[t] for row in group], lane)):
                    mixed[(rb ^ t) * 8 + j, part, t * LANES : (t + 1) * LANES] = value
            next(beside, None)
    for _ in beside:
        pass


def propagate(grid, depth, turn, mask, speed):
    plane = jax.ShapeDtypeStruct((ROWS, COLS), jnp.int32)
    return pl.pallas_call(
        propagate_kernel,
        out_shape=[
            jax.ShapeDtypeStruct((ROWS, PAD, COLS), jnp.float32),
            jax.ShapeDtypeStruct((4, PAD, LANES), jnp.float32),
            jax.ShapeDtypeStruct((4, COLS), jnp.float32),
            plane,
            plane,
            jax.ShapeDtypeStruct((8, COLS), jnp.float32),
            jax.ShapeDtypeStruct((1,), jnp.int32),
        ],
        in_specs=[VMEM, VMEM, VMEM, VMEM, SMEM],
        out_specs=[VMEM] * 6 + [SMEM],
        compiler_params=PARAMS,
        cost_estimate=pl.CostEstimate(flops=20000000, bytes_accessed=4000000, transcendentals=0),
        name="propagate",
    )(grid, depth, turn, mask, speed)


SHORT = 112
KINDS = ((2, SHORT), (3, 0), (4, 0))


def slots_of(kind):
    return kind[0] + (kind[1] > 0)


def block_rows(kind):
    return (24 * slots_of(kind) + 3 * kind[0] + 7) // 8 * 8


def tuck(row):
    spare = iota((8, LANES), 0) * 16 + (iota((8, LANES), 1) & 15)
    return lane_gather(jnp.broadcast_to(row, (8, LANES)), spare)


def untuck(rows):
    lane = iota((8, LANES), 1)
    value = lane_gather(rows, SHORT + (lane & 15))
    value = jnp.where(iota((8, LANES), 0) == lane >> 4, value, 0.0)
    for step in (4, 2, 1):
        value = value + pltpu.roll(value, step, axis=0)
    return value


def compact_kernel(kind, mixed, from_pair, from_other, edge_depth, halo_coef, pick, out, terms, fixed, spare, tails):
    lane = iota((8, LANES), 1)
    strip = lane >> 4
    back, back_two, ahead, ahead_two = [wide(halo_coef[i]) for i in range(4)]
    odd = lax.rem(lax.axis_index("tile"), 2) == 1
    low = [jnp.where(odd, from_pair[i], from_other[i]) for i in range(2)]
    high = [jnp.where(odd, from_other[i], from_pair[i]) for i in range(2)]
    terms[0] = edge_depth[0:1, :] * (back * low[1] + back_two * low[0])
    terms[1] = edge_depth[1:2, :] * (back_two * low[1])
    terms[2] = edge_depth[2:3, :] * (ahead_two * high[0])
    terms[3] = edge_depth[3:4, :] * (ahead * high[0] + ahead_two * high[1])

    for g in range(4):
        for first, row, t in ((0, 0, g), (2, 6, 3 - g)):
            lanes = slice(t * LANES, (t + 1) * LANES)
            for cb in range(4):
                part = slice(cb * 8, cb * 8 + 8)
                one, two = terms[first, part, lanes], terms[first + 1, part, lanes]
                for j in range(8):
                    term = jnp.where(strip == (row + 1) ^ j, two, 0.0)
                    term = jnp.where(strip == row ^ j, one, term)
                    fixed[g * 8 + j, first // 2, part, :] = mixed[g * 8 + j, part, lanes] - term

    whole, short = kind

    def load(d, cb, t):
        part = slice(cb * 8, cb * 8 + 8)
        if t == d // 8:
            return fixed[d, 0, part, :]
        if t == 3 - d // 8:
            return fixed[d, 1, part, :]
        return mixed[d, part, t * LANES : (t + 1) * LANES]

    def index_of(d, slot):
        index = jnp.broadcast_to(pick[d : d + 1, slot * LANES : (slot + 1) * LANES], (8, LANES))
        return index & (LANES - 1), [index >> 7 == t for t in range(TILES)]

    def picked(d, cb, slot, index, among):
        total = lane_gather(load(d, cb, slot), index)
        for source in range(slot + 1, TILES):
            value = lane_gather(load(d, cb, source), index)
            total = jnp.where(among[source], value, total)
        return total

    if short:
        for d in range(OWNERS):
            tails[d] = picked(d, 3, whole, *index_of(d, whole))
        for d in range(OWNERS):
            for cb in range(3):
                spare[d, cb] = tuck(tails[d, cb : cb + 1, :])

    for d in range(OWNERS):
        for slot in range(slots_of(kind)):
            index = index_of(d, slot)
            for cb in range(4 if slot < whole else 3):
                value = picked(d, cb, slot, *index)
                if slot >= whole:
                    value = jnp.where(lane < SHORT, value, spare[d, cb])
                if cb < 3:
                    out[d, slot * 24 + cb * 8 : slot * 24 + cb * 8 + 8, :] = value
                else:
                    row = 24 * slots_of(kind) + 3 * slot
                    out[d, row : row + 3, :] = value[0:3]


def compact(kind, mixed, from_pair, from_other, edge_depth, halo_coef, pick):
    return pl.pallas_call(
        functools.partial(compact_kernel, kind),
        out_shape=jax.ShapeDtypeStruct((OWNERS, block_rows(kind), LANES), jnp.float32),
        in_specs=[VMEM] * 6,
        out_specs=VMEM,
        scratch_shapes=[
            pltpu.VMEM((4, PAD, COLS), jnp.float32),
            pltpu.VMEM((OWNERS, 2, PAD, LANES), jnp.float32),
            pltpu.VMEM((OWNERS, 3, 8, LANES), jnp.float32),
            pltpu.VMEM((OWNERS, 8, LANES), jnp.float32),
        ],
        compiler_params=PARAMS,
        cost_estimate=pl.CostEstimate(flops=5000000, bytes_accessed=4000000, transcendentals=0),
        name="compact",
    )(mixed, from_pair, from_other, edge_depth, halo_coef, pick)


def runs():
    found = []
    for s in range(OWNERS):
        k = 0
        while k < HELD:
            c = s * HELD + k
            end = min(24 if k < 24 else HELD, k + NTH - c % NTH)
            found.append((s, k, end - k, c))
            k = end
    return found


def columns(vector):
    pieces = []
    for begin in range(0, vector.shape[0], LANES):
        size = min(LANES, vector.shape[0] - begin)
        row = jnp.broadcast_to(vector[begin : begin + size][None, :], (8, size))
        if size < LANES:
            row = jnp.concatenate([row, jnp.zeros((8, LANES - size), jnp.float32)], axis=1)
        column = jnp.transpose(row)[:size, 0:1]
        pieces.append(jnp.broadcast_to(column, (size, LANES)))
    return pieces


def source_kernel(
    kind, points, turn_own, refraction, growth, dissipation, first_far, second_far, out,
    grid, turned, low, pair,
):
    first, second = first_far, second_far
    whole = kind[0]
    tiles = slots_of(kind)
    ncomp = low.shape[0]
    nfreq = ncomp // NTH
    width = NTH + 4
    for slot in range(tiles):
        lanes = slice(slot * LANES, (slot + 1) * LANES)
        for s, k, size, c in runs():
            to = c // NTH * width + 2 + c % NTH
            if k >= 24 and slot >= whole:
                for i in range(k - 24, k - 24 + size):
                    row = slot * 24 + i * 8
                    grid[slot, to : to + 1, :] = untuck(points[s, row : row + 8, :])[0:1]
                    to += 1
                continue
            row = slot * 24 + k if k < 24 else 24 * tiles + 3 * slot + k - 24
            grid[slot, to : to + size, :] = points[s, row : row + size, :]
        for f in range(nfreq):
            base = f * width
            grid[slot, base : base + 2, :] = grid[slot, base + NTH : base + NTH + 2, :]
            grid[slot, base + NTH + 2 : base + NTH + 4, :] = grid[slot, base + 2 : base + 4, :]
        turn_row = jnp.broadcast_to(turn_own[0:1, lanes], (8, LANES))
        up = turn_row >= 0.0
        sixth = turn_row / 6.0
        by_turn = [
            sixth * jnp.where(up, 3.0, -3.0),
            sixth * jnp.where(up, 2.0, 6.0),
            sixth * jnp.where(up, -6.0, -2.0),
            jnp.where(up, sixth, -sixth),
        ]
        for f in range(nfreq):
            base = f * width
            c0, ca, cb, cf = [c * refraction[f] for c in by_turn]
            for begin in range(0, NTH, 8):
                size = min(8, NTH - begin)
                at = base + 2 + begin

                def near(step):
                    return grid[slot, at + step : at + step + size, :]

                centre = near(0)
                total = c0[:size] * centre + ca[:size] * near(1) + cb[:size] * near(-1)
                total += cf[:size] * jnp.where(up[:size], near(-2), near(2))
                to = f * NTH + begin
                turned[slot, to : to + size, :] = centre - total

    energy = []
    for slot in range(tiles):
        value = turned[slot]
        low[:, slot * LANES : (slot + 1) * LANES] = value.astype(jnp.bfloat16)
        energy.append(jnp.sum(value, axis=0, keepdims=True) / ncomp)
    keep = [1.0 + 0.2 * column for column in columns(growth)]
    lose = [0.2 * column for column in columns(dissipation)]
    partner = jnp.dot(first[...], low[...], preferred_element_type=jnp.float32)
    for slot in range(tiles):
        lanes = slice(slot * LANES, (slot + 1) * LANES)
        pair[:, lanes] = (turned[slot] * partner[:, lanes]).astype(jnp.bfloat16)
    nonlinear = jnp.dot(second[...], pair[...], preferred_element_type=jnp.float32)
    for slot in range(tiles):
        lanes = slice(slot * LANES, (slot + 1) * LANES)
        for begin in range(0, ncomp, LANES):
            part = slice(begin, min(begin + LANES, ncomp))
            scale = keep[begin // LANES] - lose[begin // LANES] * energy[slot]
            turned[slot, part, :] = turned[slot, part, :] * scale + 0.2 * nonlinear[part, lanes]
    lane = iota((8, LANES), 1)
    for s in range(OWNERS):
        for slot in range(tiles):
            c = s * HELD
            if slot < whole:
                out[s, slot * 24 : slot * 24 + 24, :] = turned[slot, c : c + 24, :]
                row = 24 * tiles + 3 * slot
                out[s, row : row + 3, :] = turned[slot, c + 24 : c + HELD, :]
                continue
            for cb in range(3):
                value = turned[slot, c + cb * 8 : c + cb * 8 + 8, :]
                spare = tuck(turned[slot, c + 24 + cb : c + 25 + cb, :])
                row = slot * 24 + cb * 8
                out[s, row : row + 8, :] = jnp.where(lane < SHORT, value, spare)


def sources(kind, points, turn_own, refraction, growth, dissipation, first, second):
    ncomp = first.shape[0]
    tiles = slots_of(kind)
    lanes = tiles * LANES
    return pl.pallas_call(
        functools.partial(source_kernel, kind),
        out_shape=jax.ShapeDtypeStruct(points.shape, jnp.float32),
        in_specs=[VMEM, VMEM, SMEM, VMEM, VMEM, VMEM, VMEM],
        out_specs=VMEM,
        scratch_shapes=[
            pltpu.VMEM((tiles, ncomp // NTH * (NTH + 4), LANES), jnp.float32),
            pltpu.VMEM((tiles, ncomp, LANES), jnp.float32),
            pltpu.VMEM((ncomp, lanes), jnp.bfloat16),
            pltpu.VMEM((ncomp, lanes), jnp.bfloat16),
        ],
        compiler_params=PARAMS,
        cost_estimate=pl.CostEstimate(
            flops=4 * ncomp * ncomp * lanes, bytes_accessed=6000000, transcendentals=0
        ),
        name="sources",
    )(points, turn_own, refraction, growth, dissipation, first, second)


def expand_kernel(kind, result, rank, field, last):
    whole, short = kind
    slots = slots_of(kind)
    tail_rows = (3 * whole + 7) // 8 * 8
    row_at = iota((8, LANES), 0)

    def short_step(d):
        row = whole * 24
        parts = [untuck(result[d, row + cb * 8 : row + cb * 8 + 8, :]) for cb in range(3)]
        value = jnp.where(row_at == 1, parts[1], parts[0])
        last[d] = jnp.where(row_at == 2, parts[2], value)

    def value_of(d, cb, slot):
        if cb < 3:
            return result[d, slot * 24 + cb * 8 : slot * 24 + cb * 8 + 8, :]
        if slot >= whole:
            return last[d]
        tail = result[d, 24 * slots : 24 * slots + tail_rows, :]
        return pltpu.roll(tail, (tail_rows - 3 * slot) % tail_rows, axis=0)[0:8]

    def owner_cells(d, t):
        index = jnp.broadcast_to(rank[d : d + 1, t * LANES : (t + 1) * LANES], (8, LANES))
        land = index < 0
        among = [index >> 7 == slot for slot in range(slots)]
        index = index & (LANES - 1)
        cells = []
        for cb in range(4):
            total = lane_gather(value_of(d, cb, 0), index)
            for slot in range(1, min(t + 1, slots)):
                total = jnp.where(among[slot], lane_gather(value_of(d, cb, slot), index), total)
            cells.append(jnp.where(land, 0.0, total))
        return cells

    if short:
        for d in range(OWNERS):
            short_step(d)
    lane = iota((8, LANES), 1)
    for g in range(4):
        for t in range(TILES):
            cells = [owner_cells(g * 8 + j, t) for j in range(8)]
            rows = slice((g ^ t) * 8, (g ^ t) * 8 + 8)
            for cb in range(4):
                size = min(8, HELD - cb * 8)
                block = butterfly([cell[cb] for cell in cells], lane)
                block = jnp.swapaxes(jnp.stack(block), 0, 1)
                field[cb * 8 : cb * 8 + size, rows, t * LANES : (t + 1) * LANES] = block[0:size]


def expand(kind, result, rank):
    return pl.pallas_call(
        functools.partial(expand_kernel, kind),
        out_shape=jax.ShapeDtypeStruct((HELD, ROWS, COLS), jnp.float32),
        in_specs=[VMEM] * 2,
        out_specs=VMEM,
        scratch_shapes=[pltpu.VMEM((OWNERS, 8, LANES), jnp.float32)],
        compiler_params=PARAMS,
        cost_estimate=pl.CostEstimate(flops=5000000, bytes_accessed=4000000, transcendentals=0),
        name="expand",
    )(result, rank)


def finish_kernel(field, out, leaving):
    copies = []
    for cb in range(4):
        part = slice(cb * 8, min(cb * 8 + 8, HELD))
        copies.append(pltpu.make_async_copy(field.at[part], out.at[part], leaving.at[cb]))
        copies[cb].start()
    for copy in copies:
        copy.wait()


def finish(field):
    return pl.pallas_call(
        finish_kernel,
        out_shape=jax.ShapeDtypeStruct((HELD, ROWS, COLS), jnp.float32),
        in_specs=[VMEM],
        out_specs=ANY,
        scratch_shapes=[pltpu.SemaphoreType.DMA((4,))],
        compiler_params=PARAMS,
        cost_estimate=pl.CostEstimate(flops=0, bytes_accessed=4000000, transcendentals=0),
        name="finish",
    )(field)


def exchange(blocks):
    return lax.all_to_all(blocks, "comp", split_axis=0, concat_axis=0, tiled=True)


def shards(
    spectrum, speed, depth, turn, sea_mask, refraction, growth, dissipation, quad_first, quad_second
):
    count = lax.axis_size("tile")

    def swap(rows, begin):
        pairs = [(i, i + 1) for i in range(begin, count - 1, 2)]
        return lax.ppermute(rows, "tile", pairs + [(j, i) for i, j in pairs])

    grid, to_pair, to_other = prepare(spectrum)
    from_pair = swap(to_pair, 0)
    from_other = swap(to_other, 1)
    mixed, halo_coef, edge_depth, pick, rank, turn_own, chosen = propagate(
        grid, depth, turn, sea_mask, speed
    )

    def rest(kind):
        def run(mixed, from_pair, from_other):
            sent = compact(kind, mixed, from_pair, from_other, edge_depth, halo_coef, pick)
            points = exchange(sent)
            result = sources(
                kind, points, turn_own, refraction, growth, dissipation, quad_first, quad_second
            )
            return expand(kind, exchange(result), rank)

        return run

    return finish(lax.switch(chosen[0], [rest(kind) for kind in KINDS], mixed, from_pair, from_other))


def solution(mesh):
    in_specs = (
        P("comp", "tile", None),
        P("comp"),
        P("tile", None),
        P("tile", None),
        P("tile", None),
        P(),
        P(),
        P(),
        P(),
        P(),
    )
    out_specs = P("comp", "tile", None)
    return jax.shard_map(shards, mesh=mesh, in_specs=in_specs, out_specs=out_specs, check_vma=False)
```

```python
import functools
import math

import jax
import jax.numpy as jnp
from jax import lax
from jax.experimental import pallas as pl
from jax.experimental.pallas import tpu as pltpu
from jax.sharding import PartitionSpec as P

NTH = 36
HELD = 27
PAD = 32
ROWS = 32
COLS = 512
OWNERS = 32
LANES = 128
TILES = COLS // LANES
VMEM = pl.BlockSpec(memory_space=pltpu.VMEM)
SMEM = pl.BlockSpec(memory_space=pltpu.SMEM)
ANY = pl.BlockSpec(memory_space=pl.ANY)
PARAMS = pltpu.CompilerParams(vmem_limit_bytes=24 * 2**20)


def iota(shape, dim):
    return lax.broadcasted_iota(jnp.int32, shape, dim)


def lane_gather(values, index):
    return jnp.take_along_axis(values, index, axis=1, mode="promise_in_bounds")


def wide(coef):
    return jnp.concatenate([coef] * TILES, axis=1)


def butterfly(rows, lane):
    for step, bit in ((1, 16), (2, 32), (4, 64)):
        swap = (lane & bit) != 0
        rows = [jnp.where(swap, rows[j ^ step], rows[j]) for j in range(8)]
    return rows


def mixed_plane(plane):
    lane = iota((ROWS, LANES), 1)
    row = iota((ROWS, LANES), 0)
    pieces = []
    for t in range(TILES):
        block = plane[:, t * LANES : (t + 1) * LANES]
        block = jnp.concatenate([block[(g ^ t) * 8 : (g ^ t) * 8 + 8] for g in range(4)], axis=0)
        for step, bit in ((1, 16), (2, 32), (4, 64)):
            swapped = jnp.where(
                (row & step) != 0,
                pltpu.roll(block, step, axis=0),
                pltpu.roll(block, ROWS - step, axis=0),
            )
            block = jnp.where((lane & bit) != 0, swapped, block)
        pieces.append(block)
    return jnp.concatenate(pieces, axis=1)


def prepare_kernel(spec, grid, to_pair, to_other):
    for cb in range(4):
        part = slice(cb * 8, cb * 8 + 8)
        size = min(8, HELD - cb * 8)
        for rb in range(4):
            block = spec[cb * 8 : cb * 8 + size, rb * 8 : rb * 8 + 8, :]
            if size < 8:
                block = jnp.concatenate(
                    [block, jnp.zeros((8 - size, 8, COLS), jnp.float32)], axis=0
                )
            grid[rb * 8 : rb * 8 + 8, part, :] = jnp.swapaxes(block, 0, 1)
    odd = lax.rem(lax.axis_index("tile"), 2)
    to_pair[...] = grid[pl.ds((1 - odd) * (ROWS - 2), 2), :, :]
    to_other[...] = grid[pl.ds(odd * (ROWS - 2), 2), :, :]


def prepare(spectrum):
    edge = jax.ShapeDtypeStruct((2, PAD, COLS), jnp.float32)
    return pl.pallas_call(
        prepare_kernel,
        out_shape=[jax.ShapeDtypeStruct((ROWS, PAD, COLS), jnp.float32), edge, edge],
        in_specs=[VMEM],
        out_specs=[VMEM] * 3,
        compiler_params=PARAMS,
        cost_estimate=pl.CostEstimate(flops=2000000, bytes_accessed=4000000, transcendentals=0),
        name="prepare",
    )(spectrum)


def index_steps(me, turn, mask, pick, rank, turn_own, chosen):
    sea = mixed_plane(mask[...])
    yield
    column = iota((ROWS, COLS), 1)
    count = sea
    step = 1
    while step < COLS:
        count = count + jnp.where(column >= step, pltpu.roll(count, step, axis=1), 0)
        step *= 2
        if step <= LANES:
            yield
    largest = jnp.max(count)
    kind = jnp.int32(0)
    for whole, short in KINDS[:-1]:
        kind += (largest > whole * LANES + short).astype(jnp.int32)
    chosen[0] = kind
    place = count - 1
    rank[...] = jnp.where(sea > 0, place, -1)
    entry = jnp.where(sea > 0, column * COLS + (column - place), -1)
    step = 1
    while step < COLS:
        other = pltpu.roll(entry, COLS - step, axis=1)
        arrives = (other >= 0) & ((other & step) != 0)
        stays = (entry >= 0) & ((entry & step) == 0)
        entry = jnp.where(arrives, other, jnp.where(stays, entry, -1))
        step *= 2
        if step <= LANES:
            yield
    entry = jnp.where(entry >= 0, entry >> 9, 0)
    pick[...] = entry
    mine = iota((ROWS, COLS), 0) == me
    own_turn = jnp.sum(jnp.where(mine, mixed_plane(turn[...]), 0.0), axis=0, keepdims=True)
    own_pick = jnp.sum(jnp.where(mine, entry, 0), axis=0, keepdims=True)
    for t in range(TILES):
        index = jnp.broadcast_to(own_pick[:, t * LANES : (t + 1) * LANES], (8, LANES))
        total = jnp.zeros((8, LANES), jnp.float32)
        for source in range(TILES):
            own = jnp.broadcast_to(own_turn[:, source * LANES : (source + 1) * LANES], (8, LANES))
            value = lane_gather(own, index & (LANES - 1))
            total = jnp.where(index >> 7 == source, value, total)
        turn_own[:, t * LANES : (t + 1) * LANES] = total
    yield


def shifted(tiles, lane, far_lane, take_back, take_ahead):
    ahead = [pltpu.roll(v, LANES - 1, axis=1) for v in tiles] + [0.0]
    back = [0.0] + [pltpu.roll(v, 1, axis=1) for v in tiles]
    far = [0.0] + [lane_gather(v, far_lane) for v in tiles] + [0.0]
    return [
        (
            jnp.where(lane < LANES - 1, ahead[t], ahead[t + 1]),
            jnp.where(lane >= 1, back[t + 1], back[t]),
            jnp.where(take_back, far[t], jnp.where(take_ahead, far[t + 2], far[t + 1])),
        )
        for t in range(TILES)
    ]


def propagate_kernel(
    grid, depth, turn, mask, speed, mixed, halo_coef, edge_depth, pick, rank, turn_own, chosen
):
    me = lax.axis_index("comp")
    beside = index_steps(me, turn, mask, pick, rank, turn_own, chosen)
    sub = iota((PAD, LANES), 0)
    speeds = jnp.zeros((PAD, LANES), jnp.float32)
    for k in range(HELD):
        speeds = jnp.where(sub == k, speed[k], speeds)
    theta = (2.0 * math.pi / NTH) * lax.rem(me * HELD + sub, NTH).astype(jnp.float32)

    def taps(velocity):
        up = velocity >= 0.0
        sixth = velocity / 6.0
        return (
            sixth * jnp.where(up, 3.0, -3.0),
            sixth * jnp.where(up, 2.0, 6.0),
            sixth * jnp.where(up, -6.0, -2.0),
            jnp.where(up, sixth, -sixth),
            up,
        )

    x_centre, x_ahead, x_back, x_far, x_up = taps(speeds * jnp.cos(theta))
    y_centre, y_ahead, y_back, y_far, y_up = taps(speeds * jnp.sin(theta))
    edge_depth[0:2, :] = depth[0:2, :]
    edge_depth[2:4, :] = depth[ROWS - 2 : ROWS, :]
    halo_coef[0] = y_back
    halo_coef[1] = jnp.where(y_up, y_far, 0.0)
    halo_coef[2] = y_ahead
    halo_coef[3] = jnp.where(y_up, 0.0, y_far)
    centre_coef = x_centre + y_centre

    lane = iota((8, LANES), 1)
    for cb in range(4):
        part = slice(cb * 8, cb * 8 + 8)
        c0, xa, xb, xf, xu, ya, yb, yf, yu = [
            c[part]
            for c in (centre_coef, x_ahead, x_back, x_far, x_up, y_ahead, y_back, y_far, y_up)
        ]

        far_from = (
            (lane + jnp.where(xu, LANES - 2, 2)) & (LANES - 1),
            xu & (lane < 2),
            jnp.logical_not(xu) & (lane >= LANES - 2),
        )

        def row_step(r, rows, depth_row):
            results = []
            centre = [grid[r, part, t * LANES : (t + 1) * LANES] for t in range(TILES)]

            def near(i, t):
                if not 0 <= rows + i < ROWS:
                    return jnp.zeros((8, LANES), jnp.float32)
                return grid[r + i, part, t * LANES : (t + 1) * LANES]

            for t, (ahead, back, far) in enumerate(shifted(centre, lane, *far_from)):
                total = c0 * centre[t] + xa * ahead + xb * back
                total += xf * far
                total += ya * near(1, t) + yb * near(-1, t)
                total += yf * jnp.where(yu, near(-2, t), near(2, t))
                lanes = slice(t * LANES, (t + 1) * LANES)
                results.append(centre[t] - depth_row[:, lanes] * total)
            return results

        for rb in range(ROWS // 8):
            depths = depth[rb * 8 : rb * 8 + 8, :]
            group = [row_step(rb * 8 + i, rb * 8 + i, depths[i : i + 1, :]) for i in range(8)]
            for t in range(TILES):
                for j, value in enumerate(butterfly([row[t] for row in group], lane)):
                    mixed[(rb ^ t) * 8 + j, part, t * LANES : (t + 1) * LANES] = value
            next(beside, None)
    for _ in beside:
        pass


def propagate(grid, depth, turn, mask, speed):
    plane = jax.ShapeDtypeStruct((ROWS, COLS), jnp.int32)
    return pl.pallas_call(
        propagate_kernel,
        out_shape=[
            jax.ShapeDtypeStruct((ROWS, PAD, COLS), jnp.float32),
            jax.ShapeDtypeStruct((4, PAD, LANES), jnp.float32),
            jax.ShapeDtypeStruct((4, COLS), jnp.float32),
            plane,
            plane,
            jax.ShapeDtypeStruct((8, COLS), jnp.float32),
            jax.ShapeDtypeStruct((1,), jnp.int32),
        ],
        in_specs=[VMEM, VMEM, VMEM, VMEM, SMEM],
        out_specs=[VMEM] * 6 + [SMEM],
        compiler_params=PARAMS,
        cost_estimate=pl.CostEstimate(flops=20000000, bytes_accessed=4000000, transcendentals=0),
        name="propagate",
    )(grid, depth, turn, mask, speed)


SHORT = 112
KINDS = ((2, SHORT), (3, 0), (4, 0))


def slots_of(kind):
    return kind[0] + (kind[1] > 0)


def block_rows(kind):
    return (24 * slots_of(kind) + 3 * kind[0] + 7) // 8 * 8


def tuck(row):
    spare = iota((8, LANES), 0) * 16 + (iota((8, LANES), 1) & 15)
    return lane_gather(jnp.broadcast_to(row, (8, LANES)), spare)


def untuck(rows):
    lane = iota((8, LANES), 1)
    value = lane_gather(rows, SHORT + (lane & 15))
    value = jnp.where(iota((8, LANES), 0) == lane >> 4, value, 0.0)
    for step in (4, 2, 1):
        value = value + pltpu.roll(value, step, axis=0)
    return value


def compact_kernel(kind, mixed, from_pair, from_other, edge_depth, halo_coef, pick, out, terms, fixed, spare, tails):
    lane = iota((8, LANES), 1)
    strip = lane >> 4
    back, back_two, ahead, ahead_two = [wide(halo_coef[i]) for i in range(4)]
    odd = lax.rem(lax.axis_index("tile"), 2) == 1
    low = [jnp.where(odd, from_pair[i], from_other[i]) for i in range(2)]
    high = [jnp.where(odd, from_other[i], from_pair[i]) for i in range(2)]
    terms[0] = edge_depth[0:1, :] * (back * low[1] + back_two * low[0])
    terms[1] = edge_depth[1:2, :] * (back_two * low[1])
    terms[2] = edge_depth[2:3, :] * (ahead_two * high[0])
    terms[3] = edge_depth[3:4, :] * (ahead * high[0] + ahead_two * high[1])

    for g in range(4):
        for first, row, t in ((0, 0, g), (2, 6, 3 - g)):
            lanes = slice(t * LANES, (t + 1) * LANES)
            for cb in range(4):
                part = slice(cb * 8, cb * 8 + 8)
                one, two = terms[first, part, lanes], terms[first + 1, part, lanes]
                for j in range(8):
                    term = jnp.where(strip == (row + 1) ^ j, two, 0.0)
                    term = jnp.where(strip == row ^ j, one, term)
                    fixed[g * 8 + j, first // 2, part, :] = mixed[g * 8 + j, part, lanes] - term

    whole, short = kind

    def load(d, cb, t):
        part = slice(cb * 8, cb * 8 + 8)
        if t == d // 8:
            return fixed[d, 0, part, :]
        if t == 3 - d // 8:
            return fixed[d, 1, part, :]
        return mixed[d, part, t * LANES : (t + 1) * LANES]

    def index_of(d, slot):
        index = jnp.broadcast_to(pick[d : d + 1, slot * LANES : (slot + 1) * LANES], (8, LANES))
        return index & (LANES - 1), [index >> 7 == t for t in range(TILES)]

    def picked(d, cb, slot, index, among):
        total = lane_gather(load(d, cb, slot), index)
        for source in range(slot + 1, TILES):
            value = lane_gather(load(d, cb, source), index)
            total = jnp.where(among[source], value, total)
        return total

    if short:
        for d in range(OWNERS):
            tails[d] = picked(d, 3, whole, *index_of(d, whole))
        for d in range(OWNERS):
            for cb in range(3):
                spare[d, cb] = tuck(tails[d, cb : cb + 1, :])

    for d in range(OWNERS):
        for slot in range(slots_of(kind)):
            index = index_of(d, slot)
            for cb in range(4 if slot < whole else 3):
                value = picked(d, cb, slot, *index)
                if slot >= whole:
                    value = jnp.where(lane < SHORT, value, spare[d, cb])
                if cb < 3:
                    out[d, slot * 24 + cb * 8 : slot * 24 + cb * 8 + 8, :] = value
                else:
                    row = 24 * slots_of(kind) + 3 * slot
                    out[d, row : row + 3, :] = value[0:3]


def compact(kind, mixed, from_pair, from_other, edge_depth, halo_coef, pick):
    return pl.pallas_call(
        functools.partial(compact_kernel, kind),
        out_shape=jax.ShapeDtypeStruct((OWNERS, block_rows(kind), LANES), jnp.float32),
        in_specs=[VMEM] * 6,
        out_specs=VMEM,
        scratch_shapes=[
            pltpu.VMEM((4, PAD, COLS), jnp.float32),
            pltpu.VMEM((OWNERS, 2, PAD, LANES), jnp.float32),
            pltpu.VMEM((OWNERS, 3, 8, LANES), jnp.float32),
            pltpu.VMEM((OWNERS, 8, LANES), jnp.float32),
        ],
        compiler_params=PARAMS,
        cost_estimate=pl.CostEstimate(flops=5000000, bytes_accessed=4000000, transcendentals=0),
        name="compact",
    )(mixed, from_pair, from_other, edge_depth, halo_coef, pick)


def runs():
    found = []
    for s in range(OWNERS):
        k = 0
        while k < HELD:
            c = s * HELD + k
            end = min(24 if k < 24 else HELD, k + NTH - c % NTH)
            found.append((s, k, end - k, c))
            k = end
    return found


def columns(vector):
    pieces = []
    for begin in range(0, vector.shape[0], LANES):
        size = min(LANES, vector.shape[0] - begin)
        row = jnp.broadcast_to(vector[begin : begin + size][None, :], (8, size))
        if size < LANES:
            row = jnp.concatenate([row, jnp.zeros((8, LANES - size), jnp.float32)], axis=1)
        column = jnp.transpose(row)[:size, 0:1]
        pieces.append(jnp.broadcast_to(column, (size, LANES)))
    return pieces


def source_kernel(
    kind, points, turn_own, refraction, growth, dissipation, first_far, second_far, out,
    grid, turned, low, pair,
):
    first, second = first_far, second_far
    whole = kind[0]
    tiles = slots_of(kind)
    ncomp = low.shape[0]
    nfreq = ncomp // NTH
    width = NTH + 4
    for slot in range(tiles):
        lanes = slice(slot * LANES, (slot + 1) * LANES)
        for s, k, size, c in runs():
            to = c // NTH * width + 2 + c % NTH
            if k >= 24 and slot >= whole:
                for i in range(k - 24, k - 24 + size):
                    row = slot * 24 + i * 8
                    grid[slot, to : to + 1, :] = untuck(points[s, row : row + 8, :])[0:1]
                    to += 1
                continue
            row = slot * 24 + k if k < 24 else 24 * tiles + 3 * slot + k - 24
            grid[slot, to : to + size, :] = points[s, row : row + size, :]
        for f in range(nfreq):
            base = f * width
            grid[slot, base : base + 2, :] = grid[slot, base + NTH : base + NTH + 2, :]
            grid[slot, base + NTH + 2 : base + NTH + 4, :] = grid[slot, base + 2 : base + 4, :]
        turn_row = jnp.broadcast_to(turn_own[0:1, lanes], (8, LANES))
        up = turn_row >= 0.0
        sixth = turn_row / 6.0
        by_turn = [
            sixth * jnp.where(up, 3.0, -3.0),
            sixth * jnp.where(up, 2.0, 6.0),
            sixth * jnp.where(up, -6.0, -2.0),
            jnp.where(up, sixth, -sixth),
        ]
        for f in range(nfreq):
            base = f * width
            c0, ca, cb, cf = [c * refraction[f] for c in by_turn]
            for begin in range(0, NTH, 8):
                size = min(8, NTH - begin)
                at = base + 2 + begin

                def near(step):
                    return grid[slot, at + step : at + step + size, :]

                centre = near(0)
                total = c0[:size] * centre + ca[:size] * near(1) + cb[:size] * near(-1)
                total += cf[:size] * jnp.where(up[:size], near(-2), near(2))
                to = f * NTH + begin
                turned[slot, to : to + size, :] = centre - total

    energy = []
    for slot in range(tiles):
        value = turned[slot]
        low[:, slot * LANES : (slot + 1) * LANES] = value.astype(jnp.bfloat16)
        energy.append(jnp.sum(value, axis=0, keepdims=True) / ncomp)
    keep = [1.0 + 0.2 * column for column in columns(growth)]
    lose = [0.2 * column for column in columns(dissipation)]
    partner = jnp.dot(first[...], low[...], preferred_element_type=jnp.float32)
    for slot in range(tiles):
        lanes = slice(slot * LANES, (slot + 1) * LANES)
        pair[:, lanes] = (turned[slot] * partner[:, lanes]).astype(jnp.bfloat16)
    nonlinear = jnp.dot(second[...], pair[...], preferred_element_type=jnp.float32)
    for slot in range(tiles):
        lanes = slice(slot * LANES, (slot + 1) * LANES)
        for begin in range(0, ncomp, LANES):
            part = slice(begin, min(begin + LANES, ncomp))
            scale = keep[begin // LANES] - lose[begin // LANES] * energy[slot]
            turned[slot, part, :] = turned[slot, part, :] * scale + 0.2 * nonlinear[part, lanes]
    lane = iota((8, LANES), 1)
    for s in range(OWNERS):
        for slot in range(tiles):
            c = s * HELD
            if slot < whole:
                out[s, slot * 24 : slot * 24 + 24, :] = turned[slot, c : c + 24, :]
                row = 24 * tiles + 3 * slot
                out[s, row : row + 3, :] = turned[slot, c + 24 : c + HELD, :]
                continue
            for cb in range(3):
                value = turned[slot, c + cb * 8 : c + cb * 8 + 8, :]
                spare = tuck(turned[slot, c + 24 + cb : c + 25 + cb, :])
                row = slot * 24 + cb * 8
                out[s, row : row + 8, :] = jnp.where(lane < SHORT, value, spare)


def sources(kind, points, turn_own, refraction, growth, dissipation, first, second):
    ncomp = first.shape[0]
    tiles = slots_of(kind)
    lanes = tiles * LANES
    return pl.pallas_call(
        functools.partial(source_kernel, kind),
        out_shape=jax.ShapeDtypeStruct(points.shape, jnp.float32),
        in_specs=[VMEM, VMEM, SMEM, VMEM, VMEM, VMEM, VMEM],
        out_specs=VMEM,
        scratch_shapes=[
            pltpu.VMEM((tiles, ncomp // NTH * (NTH + 4), LANES), jnp.float32),
            pltpu.VMEM((tiles, ncomp, LANES), jnp.float32),
            pltpu.VMEM((ncomp, lanes), jnp.bfloat16),
            pltpu.VMEM((ncomp, lanes), jnp.bfloat16),
        ],
        compiler_params=PARAMS,
        cost_estimate=pl.CostEstimate(
            flops=4 * ncomp * ncomp * lanes, bytes_accessed=6000000, transcendentals=0
        ),
        name="sources",
    )(points, turn_own, refraction, growth, dissipation, first, second)


def expand_kernel(kind, result, rank, field, last):
    whole, short = kind
    slots = slots_of(kind)
    tail_rows = (3 * whole + 7) // 8 * 8
    row_at = iota((8, LANES), 0)

    def short_step(d):
        row = whole * 24
        parts = [untuck(result[d, row + cb * 8 : row + cb * 8 + 8, :]) for cb in range(3)]
        value = jnp.where(row_at == 1, parts[1], parts[0])
        last[d] = jnp.where(row_at == 2, parts[2], value)

    def value_of(d, cb, slot):
        if cb < 3:
            return result[d, slot * 24 + cb * 8 : slot * 24 + cb * 8 + 8, :]
        if slot >= whole:
            return last[d]
        tail = result[d, 24 * slots : 24 * slots + tail_rows, :]
        return pltpu.roll(tail, (tail_rows - 3 * slot) % tail_rows, axis=0)[0:8]

    def owner_cells(d, t):
        index = jnp.broadcast_to(rank[d : d + 1, t * LANES : (t + 1) * LANES], (8, LANES))
        land = index < 0
        among = [index >> 7 == slot for slot in range(slots)]
        index = index & (LANES - 1)
        cells = []
        for cb in range(4):
            total = lane_gather(value_of(d, cb, 0), index)
            for slot in range(1, min(t + 1, slots)):
                total = jnp.where(among[slot], lane_gather(value_of(d, cb, slot), index), total)
            cells.append(jnp.where(land, 0.0, total))
        return cells

    if short:
        for d in range(OWNERS):
            short_step(d)
    lane = iota((8, LANES), 1)
    for g in range(4):
        for t in range(TILES):
            cells = [owner_cells(g * 8 + j, t) for j in range(8)]
            rows = slice((g ^ t) * 8, (g ^ t) * 8 + 8)
            for cb in range(4):
                size = min(8, HELD - cb * 8)
                block = butterfly([cell[cb] for cell in cells], lane)
                block = jnp.swapaxes(jnp.stack(block), 0, 1)
                field[cb * 8 : cb * 8 + size, rows, t * LANES : (t + 1) * LANES] = block[0:size]


def expand(kind, result, rank):
    return pl.pallas_call(
        functools.partial(expand_kernel, kind),
        out_shape=jax.ShapeDtypeStruct((HELD, ROWS, COLS), jnp.float32),
        in_specs=[VMEM] * 2,
        out_specs=VMEM,
        scratch_shapes=[pltpu.VMEM((OWNERS, 8, LANES), jnp.float32)],
        compiler_params=PARAMS,
        cost_estimate=pl.CostEstimate(flops=5000000, bytes_accessed=4000000, transcendentals=0),
        name="expand",
    )(result, rank)


def finish_kernel(field, out, leaving):
    copy = pltpu.make_async_copy(field, out, leaving)
    copy.start()
    copy.wait()


def finish(field):
    return pl.pallas_call(
        finish_kernel,
        out_shape=jax.ShapeDtypeStruct((HELD, ROWS, COLS), jnp.float32),
        in_specs=[VMEM],
        out_specs=ANY,
        scratch_shapes=[pltpu.SemaphoreType.DMA],
        compiler_params=PARAMS,
        cost_estimate=pl.CostEstimate(flops=0, bytes_accessed=4000000, transcendentals=0),
        name="finish",
    )(field)


def exchange(blocks):
    return lax.all_to_all(blocks, "comp", split_axis=0, concat_axis=0, tiled=True)


def shards(
    spectrum, speed, depth, turn, sea_mask, refraction, growth, dissipation, quad_first, quad_second
):
    count = lax.axis_size("tile")

    def swap(rows, begin):
        pairs = [(i, i + 1) for i in range(begin, count - 1, 2)]
        return lax.ppermute(rows, "tile", pairs + [(j, i) for i, j in pairs])

    grid, to_pair, to_other = prepare(spectrum)
    from_pair = swap(to_pair, 0)
    from_other = swap(to_other, 1)
    mixed, halo_coef, edge_depth, pick, rank, turn_own, chosen = propagate(
        grid, depth, turn, sea_mask, speed
    )

    def rest(kind):
        def run(mixed, from_pair, from_other):
            sent = compact(kind, mixed, from_pair, from_other, edge_depth, halo_coef, pick)
            points = exchange(sent)
            result = sources(
                kind, points, turn_own, refraction, growth, dissipation, quad_first, quad_second
            )
            return expand(kind, exchange(result), rank)

        return run

    return finish(lax.switch(chosen[0], [rest(kind) for kind in KINDS], mixed, from_pair, from_other))


def solution(mesh):
    in_specs = (
        P("comp", "tile", None),
        P("comp"),
        P("tile", None),
        P("tile", None),
        P("tile", None),
        P(),
        P(),
        P(),
        P(),
        P(),
    )
    out_specs = P("comp", "tile", None)
    return jax.shard_map(shards, mesh=mesh, in_specs=in_specs, out_specs=out_specs, check_vma=False)
```
